32 devices in a mesh: dom: 2 (over x), head: 16 (over z, y, core).
Axes of the slice: x: 2, y: 2, z: 4, core: 2. Of those that a mesh axis runs over, the one named last changes fastest.
Arguments:
- queries: bfloat16 [4096, 1024], P(('dom', 'head')), may hold values from -10 to 10
- key_vectors: bfloat16 [4096, 1024], P(('dom', 'head')), may hold values from -8 to 8
- value_vectors: bfloat16 [4096, 1024], P(('dom', 'head')), may hold values from -6 to 6
- block_lists: int32 [32, 12], replicated, may hold values from 0 to 31, as said below
- out_weight: bfloat16 [1024, 1024], replicated, may hold values from -0.1875 to 0.1875
Outputs:
- mixed: bfloat16 [4096, 1024], P(('dom', 'head'))
The draws below stay inside these ranges and needn't reach their ends.
Inputs may be any that keep to these rules, and one draw needn't show every extreme that they name: `block_lists`: partition p holds blocks p * 16 to (p + 1) * 16 - 1. In row b the first 4 entries are distinct blocks of b's own partition, b itself among them; the other 8 are distinct blocks of other partitions. The expander entries of one partition's query blocks fill other partitions 128 entries at a time, so each other partition receives none, 128, or one remainder, and one receives exactly 128.
All inputs are finite; a program needn't handle non-finite values.
Results may differ from the reference program's by a relative error of at most 0.0051.
Values may be sent and summed in bfloat16 or wider, within the bound.
A program may use at most 64 MiB of HBM per device.

```python
import jax
import jax.numpy as jnp
from jax import lax

D = 1024
HEADS = 16
BLK = 128
LC = 4
LE = 8
QBP = 16
NB = 32
NODES = 4096
CAPE = 128


def draw_queries(key, part):
    key = jax.random.fold_in(key, 5)
    key_parts = jax.random.split(key, 1)
    return jnp.clip(2.5 * jax.random.normal(key_parts[0], (NODES, D)), -10.0, 10.0).astype(jnp.bfloat16)


def draw_key_vectors(key, part):
    key = jax.random.fold_in(key, 7)
    key_parts = jax.random.split(key, 1)
    return jnp.clip(jax.random.normal(key_parts[0], (NODES, D)), -6.0, 6.0).astype(jnp.bfloat16)


def draw_block_lists(key, part):
    key = jax.random.fold_in(key, 11)
    partitions = NB // QBP

    def partition_lists(index_value):
        sub_key = jax.random.fold_in(key, index_value)
        key_parts = jax.random.split(sub_key, 4)
        near_offsets = jnp.concatenate([jnp.zeros((1,), jnp.int32), jax.random.permutation(key_parts[0], QBP - 1)[:LC - 1].astype(jnp.int32) + 1])
        far_offsets = jax.random.permutation(key_parts[1], QBP)[:LE].astype(jnp.int32)
        others = (index_value + 1 + jax.random.permutation(key_parts[2], partitions - 1).astype(jnp.int32)) % partitions
        slot_rank = jax.random.permutation(key_parts[3], QBP * LE).astype(jnp.int32) // CAPE
        rows_local = jnp.arange(QBP, dtype=jnp.int32)
        near_lists = index_value * QBP + (rows_local[:, None] + near_offsets[None, :]) % QBP
        far_lists = others[slot_rank].reshape(QBP, LE) * QBP + (rows_local[:, None] + far_offsets[None, :]) % QBP
        return jnp.concatenate([near_lists, far_lists], axis=1)
    return jax.vmap(partition_lists)(jnp.arange(partitions, dtype=jnp.int32)).reshape(NB, LC + LE).astype(jnp.int32)


def levels(key, dims, shards, least, largest):
    loudness, own = 1.0, jax.random.fold_in(key, 6)
    for dim, shards_of in shards:
        heights = jnp.exp(jax.random.uniform(jax.random.fold_in(own, dim), (shards_of,), jnp.float32, least / len(shards), largest / len(shards)))
        loudness = loudness * jnp.repeat(heights, dims[dim] // shards_of).reshape([-1 if axis == dim else 1 for axis in range(len(dims))])
    return loudness


def scatter_about(rng, dims, spread, bound, pieces=(), held_as=jnp.bfloat16):
    result = spread * jax.random.normal(rng, dims, jnp.float32)
    if pieces:
        result = result * levels(rng, dims, pieces, -0.22, 0.18)
    return jnp.clip(result, -bound, bound).astype(held_as)


def setup_inputs(seed: int = 0) -> dict:
    keys = jax.random.split(jax.random.key(seed), 6)
    return {
        "queries": draw_queries(jax.random.fold_in(keys[5], 71), 0),
        "key_vectors": draw_key_vectors(jax.random.fold_in(keys[5], 71), 0),
        "value_vectors": scatter_about(keys[2], (NODES, D), 1.0, 6.0, ((0, 32),)),
        "block_lists": draw_block_lists(jax.random.fold_in(keys[5], 71), 0),
        "out_weight": scatter_about(keys[4], (D, D), D ** -0.5, 0.1875),
    }


def reference(queries, key_vectors, value_vectors, block_lists, out_weight):
    head_dim = D // HEADS
    listed_count = LC + LE
    query_blocks = queries.reshape(NB, BLK, HEADS, head_dim)
    key_blocks = key_vectors.reshape(NB, BLK, HEADS, head_dim)
    value_blocks = value_vectors.reshape(NB, BLK, HEADS, head_dim)

    def block_pass(operands):
        query_block, listed = operands
        near_keys = key_blocks[listed].astype(jnp.float32)
        near_values = value_blocks[listed].astype(jnp.float32)
        scores = jnp.einsum("qhd,lkhd->qhlk", query_block.astype(jnp.float32), near_keys, precision=lax.Precision.HIGHEST) * (head_dim ** -0.5)
        block_high = jnp.max(scores, axis=-1)
        highest = jnp.max(block_high, axis=-1, keepdims=True)
        scale_back = jnp.exp(block_high - highest)
        weights = jnp.exp(scores - block_high[..., None])
        totals = jnp.sum(scale_back * jnp.sum(weights, axis=-1), axis=-1)
        rounded = lax.optimization_barrier(weights.astype(jnp.bfloat16)).astype(jnp.float32)
        per_block = jnp.einsum("qhlk,lkhd->qhld", rounded, near_values, precision=lax.Precision.HIGHEST)
        summed = jnp.sum(per_block * scale_back[..., None], axis=2)
        return (summed / totals[..., None]).astype(jnp.bfloat16)

    attended = lax.map(block_pass, (query_blocks, block_lists))
    return jnp.dot(attended.reshape(NODES, D), out_weight, preferred_element_type=jnp.float32).astype(jnp.bfloat16)
```

```python
import functools

import jax
import jax.numpy as jnp
from jax import lax
from jax.experimental import pallas as pl
from jax.experimental.pallas import tpu as pltpu
from jax.sharding import PartitionSpec as P

D = 1024
HEADS = 16
BLK = 128
LC = 4
LE = 8


lowest_value = -1e30


def from_behind(x, axis, by):
    devices = lax.axis_size(axis)
    return lax.ppermute(x, axis, [(i, (i + by) % devices) for i in range(devices)])


def attend(query_tiles, key_tiles, value_tiles, factor):
    tiles = key_tiles.shape[0]
    heads_dev = key_tiles.shape[2]
    head_dim = key_tiles.shape[3]
    listed_count = key_tiles.shape[1] // BLK
    key_parts = key_tiles.reshape(tiles, listed_count, BLK, heads_dev, head_dim)
    value_parts = value_tiles.reshape(tiles, listed_count, BLK, heads_dev, head_dim)
    scores = (
        jnp.einsum("tqhd,tlkhd->tqhlk", query_tiles, key_parts, preferred_element_type=jnp.float32)
        * factor
    )
    block_high = jnp.max(scores, axis=-1)
    highest = jnp.max(block_high, axis=-1)
    scale_back = jnp.exp(block_high - highest[..., None])
    weights = jnp.exp(scores - block_high[..., None])
    totals = jnp.sum(scale_back * jnp.sum(weights, axis=-1), axis=-1)
    per_block = jnp.einsum(
        "tqhlk,tlkhd->tqhld",
        weights.astype(jnp.bfloat16),
        value_parts,
        preferred_element_type=jnp.float32,
    )
    summed = jnp.sum(per_block * scale_back[..., None], axis=3)
    return (summed, highest, totals)


def near_pass(query_blocks, key_blocks, value_blocks, near_ids, factor):
    blocks, block_rows, heads_dev, head_dim = query_blocks.shape
    groups = blocks // 4

    def group_pass(operands):
        query_group, id_group = operands
        key_group = key_blocks[id_group].reshape(4, -1, heads_dev, head_dim)
        value_group = value_blocks[id_group].reshape(4, -1, heads_dev, head_dim)
        return attend(query_group, key_group, value_group, factor)

    summed, highest, totals = lax.map(
        group_pass,
        (
            query_blocks.reshape(groups, 4, block_rows, heads_dev, head_dim),
            near_ids.reshape(groups, 4, -1),
        ),
    )
    return (
        summed.reshape(blocks, block_rows, heads_dev, head_dim),
        highest.reshape(blocks, block_rows, heads_dev),
        totals.reshape(blocks, block_rows, heads_dev),
    )


def slot_table(listed, wanted, capacity):
    places = jnp.cumsum(wanted.astype(jnp.int32)) - 1
    tile_slots = jnp.arange(capacity, dtype=jnp.int32)
    taking = wanted[None, :] & (places[None, :] == tile_slots[:, None])
    filled = jnp.any(taking, axis=1)
    entries = jnp.arange(listed.shape[0], dtype=jnp.int32)
    chosen_entry = jnp.sum(jnp.where(taking, entries[None, :], 0), axis=1)
    chosen_block = jnp.sum(jnp.where(taking, listed[None, :], 0), axis=1)
    return (filled, chosen_entry, chosen_block)


def merge_tiles(running, tile_query, filled, tile_summed, tile_highest, tile_totals):
    summed, highest, totals = running
    blocks = summed.shape[0]
    member = (tile_query[None, :] == jnp.arange(blocks, dtype=jnp.int32)[:, None]) & filled[None, :]
    reached = jnp.max(jnp.where(member[:, :, None, None], tile_highest[None], lowest_value), axis=1)
    new_highest = jnp.maximum(highest, reached)
    rescale = jnp.where(filled[:, None, None], jnp.exp(tile_highest - new_highest[tile_query]), 0.0)
    retain = jnp.exp(highest - new_highest)
    member_float = member.astype(jnp.float32)
    totals = totals * retain + jnp.einsum(
        "qt,tbh->qbh", member_float, rescale * tile_totals, precision=lax.Precision.HIGHEST
    )
    summed = summed * retain[..., None] + jnp.einsum(
        "qt,tbhd->qbhd",
        member_float,
        rescale[..., None] * tile_summed,
        precision=lax.Precision.HIGHEST,
    )
    return (summed, new_highest, totals)


def absorb(running, query_blocks, far_ids, key_blocks, value_blocks, first_block, capacity, factor):
    reach_blocks = key_blocks.shape[0]
    listed = far_ids.reshape(-1)
    wanted = (listed >= first_block) & (listed < first_block + reach_blocks)
    filled, chosen_entry, chosen_block = slot_table(listed, wanted, capacity)
    tile_query = chosen_entry // far_ids.shape[1]
    tile_key = jnp.where(filled, chosen_block - first_block, 0)
    tile_summed, tile_highest, tile_totals = attend(
        query_blocks[tile_query], key_blocks[tile_key], value_blocks[tile_key], factor
    )
    return merge_tiles(running, tile_query, filled, tile_summed, tile_highest, tile_totals)


def shards(queries, key_vectors, value_vectors, block_lists, out_weight):
    node_rows = queries.shape[0]
    head_dim = D // HEADS
    head_devices = lax.axis_size("head")
    row_split = max(1, head_devices // HEADS)
    groups = head_devices // row_split
    heads_dev = HEADS // groups
    head_cols = heads_dev * head_dim
    local_blocks = node_rows // BLK
    sub_rows = BLK // row_split
    query_parts = (
        queries.reshape(local_blocks, row_split, sub_rows, groups, head_cols)
        .transpose(0, 2, 3, 1, 4)
        .reshape(local_blocks * sub_rows, groups * row_split, head_cols)
    )

    def spread(tensor):
        return jnp.broadcast_to(
            tensor.reshape(node_rows, groups, 1, head_cols),
            (node_rows, groups, row_split, head_cols),
        ).reshape(node_rows, groups * row_split, head_cols)

    part_queries, part_keys, part_values = (
        lax.all_to_all(query_parts, "head", split_axis=1, concat_axis=0, tiled=True),
        lax.all_to_all(spread(key_vectors), "head", split_axis=1, concat_axis=0, tiled=True),
        lax.all_to_all(spread(value_vectors), "head", split_axis=1, concat_axis=0, tiled=True),
    )
    blocks = part_keys.shape[0] // BLK
    query_blocks = part_queries.reshape(blocks, sub_rows, heads_dev, head_dim)
    key_blocks = part_keys.reshape(blocks, BLK, heads_dev, head_dim)
    value_blocks = part_values.reshape(blocks, BLK, heads_dev, head_dim)
    domains = lax.axis_size("dom")
    domain_here = lax.axis_index("dom")
    score_factor = head_dim ** (-0.5)
    own_rows = lax.dynamic_slice_in_dim(block_lists, domain_here * blocks, blocks, 0)
    near_ids = own_rows[:, :LC] - domain_here * blocks
    fold_width = min(8, domains - 1)
    capacity = (blocks * LE + fold_width - 1) // fold_width
    running = near_pass(query_blocks, key_blocks, value_blocks, near_ids, score_factor)

    def visit_turn(stride, loop_state):
        visitors, partial_value = loop_state
        visitors = from_behind(visitors, "dom", 1)
        partial_value = from_behind(
            (partial_value[0], partial_value[1], partial_value[2]), "dom", 1
        )
        source = (domain_here - stride) % domains
        far_rows = lax.dynamic_slice_in_dim(block_lists, source * blocks, blocks, 0)[:, LC:]
        partial_value = absorb(
            partial_value,
            visitors,
            far_rows,
            key_blocks,
            value_blocks,
            domain_here * blocks,
            capacity,
            score_factor,
        )
        return (visitors, partial_value)

    carried = lax.fori_loop(1, domains, visit_turn, (query_blocks, running))
    running = from_behind(carried[1], "dom", 1)
    summed, highest, totals = running
    attended = (
        (summed / totals[..., None]).astype(jnp.bfloat16).reshape(blocks * sub_rows, 1, head_cols)
    )
    regrouped = lax.all_to_all(attended, "head", split_axis=0, concat_axis=1, tiled=True)
    restored = (
        regrouped.reshape(local_blocks, sub_rows, groups, row_split, head_cols)
        .transpose(0, 3, 1, 2, 4)
        .reshape(node_rows, D)
    )
    return jnp.dot(restored, out_weight, preferred_element_type=jnp.float32).astype(jnp.bfloat16)


HALF = BLK // 2
PLANE = 4


def send_peer(me, step):
    z, rest = me // PLANE, me % PLANE
    i, j = step // PLANE, step % PLANE
    to_z = ((z // 2 + 1 - i // 2) % 2) * 2 + (z + i + i // 2) % 2
    return to_z * PLANE + (rest + 1 + j) % PLANE


def recv_peer(me, step):
    z, rest = me // PLANE, me % PLANE
    i, j = step // PLANE, step % PLANE
    from_z = ((z // 2 + 1 - i // 2) % 2) * 2 + (z + i + i // 2) % 2
    return from_z * PLANE + (rest + 3 - j) % PLANE


def swap_halves(x):
    return jnp.concatenate([x[:, HALF:], x[:, :HALF]], axis=1)


def low_lanes(shape):
    return lax.broadcasted_iota(jnp.int32, shape, 1) < HALF


def fused_kernel(
    lists, q_ref, k_ref, v_ref, w_hbm, o_ref,
    kq_out, v_out, kq_near, v_near, k_far, v_far, probs, inv_total, att_out, att_in, w_ref,
    kq_send, kq_recv, v_send, v_recv, kf_send, kf_recv, vf_send, vf_recv, att_send, att_recv, w_sem,
):
    dom = lax.axis_index("dom")
    me = lax.axis_index("head")
    other = 1 - dom
    mesh_id = pl.DeviceIdType.MESH

    barrier = pltpu.get_barrier_semaphore()

    def greet(step, carry):
        pl.semaphore_signal(
            barrier, inc=1, device_id=(dom, send_peer(me, step)), device_id_type=mesh_id
        )
        return carry

    lax.fori_loop(0, HEADS - 1, greet, 0)
    pl.semaphore_signal(barrier, inc=1, device_id=(other, me), device_id_type=mesh_id)

    w_copy = pltpu.make_async_copy(w_hbm, w_ref, w_sem)
    w_copy.start()

    low = low_lanes((HALF, BLK))

    def pack(ref, pair):
        x = ref[:, pair * BLK : (pair + 1) * BLK]
        top, bottom = x[:HALF], x[HALF:]
        return (
            jnp.where(low, top, swap_halves(bottom)),
            jnp.where(low, swap_halves(top), bottom),
        )

    for pair in range(HEADS // 2):
        for odd, packed in enumerate(pack(k_ref, pair)):
            kq_out[2 * pair + odd, :HALF, :] = packed
        for odd, packed in enumerate(pack(q_ref, pair)):
            kq_out[2 * pair + odd, HALF:, :] = packed * jnp.bfloat16(0.125)

    pl.semaphore_wait(barrier, HEADS)

    def remote(src, dst, send, recv, device):
        return pltpu.make_async_remote_copy(
            src_ref=src, dst_ref=dst, send_sem=send, recv_sem=recv,
            device_id=device, device_id_type=mesh_id,
        )

    def kq_copy(source, target):
        return remote(
            kq_out.at[target], kq_near.at[source], kq_send.at[target], kq_recv.at[source], (dom, target)
        )

    def v_copy(source, target):
        return remote(
            v_out.at[target], v_near.at[source], v_send.at[target], v_recv.at[source], (dom, target)
        )

    def kf_copy(block):
        return remote(
            kq_near.at[block, pl.ds(0, HALF)], k_far.at[block], kf_send.at[block], kf_recv.at[block],
            (other, me),
        )

    def vf_copy(block):
        return remote(
            v_near.at[block], v_far.at[block], vf_send.at[block], vf_recv.at[block], (other, me)
        )

    def att_copy(head, block):
        return remote(
            att_out.at[block], att_in.at[head], att_send.at[block], att_recv.at[head], (dom, block)
        )

    def send_kq(step, carry):
        kq_copy(me, send_peer(me, step)).start()
        return carry

    lax.fori_loop(0, HEADS - 1, send_kq, 0)
    kq_near[me] = kq_out[me]
    kf_copy(me).start()

    for pair in range(HEADS // 2):
        for odd, packed in enumerate(pack(v_ref, pair)):
            v_out[2 * pair + odd] = packed

    def send_v(step, carry):
        v_copy(me, send_peer(me, step)).start()
        return carry

    lax.fori_loop(0, HEADS - 1, send_v, 0)
    v_near[me] = v_out[me]
    vf_copy(me).start()

    def pass_k(step, carry):
        source = recv_peer(me, step)
        kq_copy(source, me).wait_recv()
        kf_copy(source).start()
        return carry

    lax.fori_loop(0, HEADS - 1, pass_k, 0)

    def await_kf(block, carry):
        kf_copy(block).wait_recv()
        return carry

    lax.fori_loop(0, HEADS, await_kf, 0)

    def score_block(block, carry):
        row = dom * HEADS + block
        keys = jnp.concatenate(
            [kq_near[lax.rem(lists[row, c], HEADS), :HALF, :] for c in range(LC)]
            + [k_far[lax.rem(lists[row, c], HEADS)] for c in range(LC, LC + LE)],
            axis=0,
        )
        packed = kq_near[block, HALF:, :]
        swapped = swap_halves(packed)
        zero = jnp.zeros_like(packed)
        rows = jnp.concatenate(
            [
                jnp.where(low, packed, zero),
                jnp.where(low, swapped, zero),
                jnp.where(low, zero, swapped),
                jnp.where(low, zero, packed),
            ],
            axis=0,
        )
        scores = lax.dot_general(
            rows, keys, (((1,), (1,)), ((), ())), preferred_element_type=jnp.float32
        )
        high = jnp.max(scores, axis=1, keepdims=True)
        high = jnp.maximum(high[:BLK], high[BLK:])
        weights = jnp.exp(scores - jnp.concatenate([high, high], axis=0))
        probs[block] = weights.astype(jnp.bfloat16)
        total = jnp.sum(weights, axis=1, keepdims=True)
        inverse = 1.0 / (total[:BLK] + total[BLK:])
        inv_total[block] = jnp.where(low, inverse[:HALF], inverse[HALF:])
        return carry

    lax.fori_loop(0, HEADS, score_block, 0)

    def pass_v(step, carry):
        source = recv_peer(me, step)
        v_copy(source, me).wait_recv()
        vf_copy(source).start()
        return carry

    lax.fori_loop(0, HEADS - 1, pass_v, 0)

    def await_vf(block, carry):
        vf_copy(block).wait_recv()
        return carry

    lax.fori_loop(0, HEADS, await_vf, 0)

    def attend_block(block):
        row = dom * HEADS + block
        values = jnp.concatenate(
            [v_near[lax.rem(lists[row, c], HEADS)] for c in range(LC)]
            + [v_far[lax.rem(lists[row, c], HEADS)] for c in range(LC, LC + LE)],
            axis=0,
        )
        summed = jnp.dot(probs[block], values, preferred_element_type=jnp.float32)
        first, second = summed[:BLK], summed[BLK:]
        packed = jnp.where(
            low,
            first[:HALF] + swap_halves(second[:HALF]),
            swap_halves(first[HALF:]) + second[HALF:],
        )
        return (packed * inv_total[block]).astype(jnp.bfloat16)

    def attend_and_send(step, carry):
        block = send_peer(me, step)
        att_out[block] = attend_block(block)
        att_copy(me, block).start()
        return carry

    lax.fori_loop(0, HEADS - 1, attend_and_send, 0)
    att_in[me] = attend_block(me)
    w_copy.wait()

    mixed = jnp.zeros((BLK, D), jnp.float32)
    for i in range(HEADS // PLANE):
        first_head = (recv_peer(me, i * PLANE) // PLANE) * PLANE
        for j in range(PLANE):
            head = first_head + j

            @pl.when(head != me)
            def _():
                att_copy(head, me).wait_recv()

        columns = []
        for j in range(0, PLANE, 2):
            even, odd = att_in[first_head + j], att_in[first_head + j + 1]
            columns.append(
                jnp.concatenate(
                    [
                        jnp.where(low, even, swap_halves(odd)),
                        jnp.where(low, swap_halves(even), odd),
                    ],
                    axis=0,
                )
            )
        attended = jnp.concatenate(columns, axis=1)
        rows_at = pl.multiple_of(first_head * HALF, PLANE * HALF)
        mixed = mixed + jnp.dot(
            attended, w_ref[pl.ds(rows_at, PLANE * HALF), :], preferred_element_type=jnp.float32
        )
    o_ref[...] = mixed.astype(o_ref.dtype)

    def settle(step, carry):
        target = send_peer(me, step)
        kq_copy(me, target).wait_send()
        v_copy(me, target).wait_send()
        att_copy(me, target).wait_send()
        return carry

    lax.fori_loop(0, HEADS - 1, settle, 0)

    def settle_far(block, carry):
        kf_copy(block).wait_send()
        vf_copy(block).wait_send()
        return carry

    lax.fori_loop(0, HEADS, settle_far, 0)


def fused_shards(queries, key_vectors, value_vectors, block_lists, out_weight):
    vmem = pl.BlockSpec(memory_space=pltpu.VMEM)
    half_blocks = pltpu.VMEM((HEADS, HALF, BLK), jnp.bfloat16)
    whole_blocks = pltpu.VMEM((HEADS, BLK, BLK), jnp.bfloat16)
    pairs = HEADS * (LC + LE) * BLK * BLK
    return pl.pallas_call(
        fused_kernel,
        out_shape=jax.ShapeDtypeStruct(queries.shape, jnp.bfloat16),
        in_specs=[
            pl.BlockSpec(memory_space=pltpu.SMEM),
            vmem,
            vmem,
            vmem,
            pl.BlockSpec(memory_space=pl.ANY),
        ],
        out_specs=vmem,
        scratch_shapes=[
            whole_blocks,
            half_blocks,
            whole_blocks,
            half_blocks,
            half_blocks,
            half_blocks,
            pltpu.VMEM((HEADS, 2 * BLK, (LC + LE) * HALF), jnp.bfloat16),
            pltpu.VMEM((HEADS, HALF, BLK), jnp.float32),
            half_blocks,
            half_blocks,
            pltpu.VMEM((D, D), jnp.bfloat16),
        ]
        + [pltpu.SemaphoreType.DMA((HEADS,))] * 10
        + [pltpu.SemaphoreType.DMA],
        compiler_params=pltpu.CompilerParams(
            collective_id=0, has_side_effects=True, vmem_limit_bytes=48 * 1024 * 1024
        ),
        cost_estimate=pl.CostEstimate(
            flops=4 * pairs * (D // HEADS) + 2 * BLK * D * D,
            bytes_accessed=4 * BLK * D * 2 + D * D * 2,
            transcendentals=pairs,
        ),
    )(block_lists, queries, key_vectors, value_vectors, out_weight)


def solution(mesh):
    in_specs = (
        P(("dom", "head"), None),
        P(("dom", "head"), None),
        P(("dom", "head"), None),
        P(),
        P(),
    )
    out_specs = P(("dom", "head"), None)
    fused_fits = mesh.shape["dom"] == 2 and mesh.shape["head"] == HEADS
    body = fused_shards if fused_fits else shards
    return jax.shard_map(body, mesh=mesh, in_specs=in_specs, out_specs=out_specs, check_vma=False)
```

```python
import functools

import jax
import jax.numpy as jnp
from jax import lax
from jax.experimental import pallas as pl
from jax.experimental.pallas import tpu as pltpu
from jax.sharding import PartitionSpec as P

D = 1024
HEADS = 16
BLK = 128
LC = 4
LE = 8


lowest_value = -1e30


def from_behind(x, axis, by):
    devices = lax.axis_size(axis)
    return lax.ppermute(x, axis, [(i, (i + by) % devices) for i in range(devices)])


def attend(query_tiles, key_tiles, value_tiles, factor):
    tiles = key_tiles.shape[0]
    heads_dev = key_tiles.shape[2]
    head_dim = key_tiles.shape[3]
    listed_count = key_tiles.shape[1] // BLK
    key_parts = key_tiles.reshape(tiles, listed_count, BLK, heads_dev, head_dim)
    value_parts = value_tiles.reshape(tiles, listed_count, BLK, heads_dev, head_dim)
    scores = (
        jnp.einsum("tqhd,tlkhd->tqhlk", query_tiles, key_parts, preferred_element_type=jnp.float32)
        * factor
    )
    block_high = jnp.max(scores, axis=-1)
    highest = jnp.max(block_high, axis=-1)
    scale_back = jnp.exp(block_high - highest[..., None])
    weights = jnp.exp(scores - block_high[..., None])
    totals = jnp.sum(scale_back * jnp.sum(weights, axis=-1), axis=-1)
    per_block = jnp.einsum(
        "tqhlk,tlkhd->tqhld",
        weights.astype(jnp.bfloat16),
        value_parts,
        preferred_element_type=jnp.float32,
    )
    summed = jnp.sum(per_block * scale_back[..., None], axis=3)
    return (summed, highest, totals)


def near_pass(query_blocks, key_blocks, value_blocks, near_ids, factor):
    blocks, block_rows, heads_dev, head_dim = query_blocks.shape
    groups = blocks // 4

    def group_pass(operands):
        query_group, id_group = operands
        key_group = key_blocks[id_group].reshape(4, -1, heads_dev, head_dim)
        value_group = value_blocks[id_group].reshape(4, -1, heads_dev, head_dim)
        return attend(query_group, key_group, value_group, factor)

    summed, highest, totals = lax.map(
        group_pass,
        (
            query_blocks.reshape(groups, 4, block_rows, heads_dev, head_dim),
            near_ids.reshape(groups, 4, -1),
        ),
    )
    return (
        summed.reshape(blocks, block_rows, heads_dev, head_dim),
        highest.reshape(blocks, block_rows, heads_dev),
        totals.reshape(blocks, block_rows, heads_dev),
    )


def slot_table(listed, wanted, capacity):
    places = jnp.cumsum(wanted.astype(jnp.int32)) - 1
    tile_slots = jnp.arange(capacity, dtype=jnp.int32)
    taking = wanted[None, :] & (places[None, :] == tile_slots[:, None])
    filled = jnp.any(taking, axis=1)
    entries = jnp.arange(listed.shape[0], dtype=jnp.int32)
    chosen_entry = jnp.sum(jnp.where(taking, entries[None, :], 0), axis=1)
    chosen_block = jnp.sum(jnp.where(taking, listed[None, :], 0), axis=1)
    return (filled, chosen_entry, chosen_block)


def merge_tiles(running, tile_query, filled, tile_summed, tile_highest, tile_totals):
    summed, highest, totals = running
    blocks = summed.shape[0]
    member = (tile_query[None, :] == jnp.arange(blocks, dtype=jnp.int32)[:, None]) & filled[None, :]
    reached = jnp.max(jnp.where(member[:, :, None, None], tile_highest[None], lowest_value), axis=1)
    new_highest = jnp.maximum(highest, reached)
    rescale = jnp.where(filled[:, None, None], jnp.exp(tile_highest - new_highest[tile_query]), 0.0)
    retain = jnp.exp(highest - new_highest)
    member_float = member.astype(jnp.float32)
    totals = totals * retain + jnp.einsum(
        "qt,tbh->qbh", member_float, rescale * tile_totals, precision=lax.Precision.HIGHEST
    )
    summed = summed * retain[..., None] + jnp.einsum(
        "qt,tbhd->qbhd",
        member_float,
        rescale[..., None] * tile_summed,
        precision=lax.Precision.HIGHEST,
    )
    return (summed, new_highest, totals)


def absorb(running, query_blocks, far_ids, key_blocks, value_blocks, first_block, capacity, factor):
    reach_blocks = key_blocks.shape[0]
    listed = far_ids.reshape(-1)
    wanted = (listed >= first_block) & (listed < first_block + reach_blocks)
    filled, chosen_entry, chosen_block = slot_table(listed, wanted, capacity)
    tile_query = chosen_entry // far_ids.shape[1]
    tile_key = jnp.where(filled, chosen_block - first_block, 0)
    tile_summed, tile_highest, tile_totals = attend(
        query_blocks[tile_query], key_blocks[tile_key], value_blocks[tile_key], factor
    )
    return merge_tiles(running, tile_query, filled, tile_summed, tile_highest, tile_totals)


def shards(queries, key_vectors, value_vectors, block_lists, out_weight):
    node_rows = queries.shape[0]
    head_dim = D // HEADS
    head_devices = lax.axis_size("head")
    row_split = max(1, head_devices // HEADS)
    groups = head_devices // row_split
    heads_dev = HEADS // groups
    head_cols = heads_dev * head_dim
    local_blocks = node_rows // BLK
    sub_rows = BLK // row_split
    query_parts = (
        queries.reshape(local_blocks, row_split, sub_rows, groups, head_cols)
        .transpose(0, 2, 3, 1, 4)
        .reshape(local_blocks * sub_rows, groups * row_split, head_cols)
    )

    def spread(tensor):
        return jnp.broadcast_to(
            tensor.reshape(node_rows, groups, 1, head_cols),
            (node_rows, groups, row_split, head_cols),
        ).reshape(node_rows, groups * row_split, head_cols)

    part_queries, part_keys, part_values = (
        lax.all_to_all(query_parts, "head", split_axis=1, concat_axis=0, tiled=True),
        lax.all_to_all(spread(key_vectors), "head", split_axis=1, concat_axis=0, tiled=True),
        lax.all_to_all(spread(value_vectors), "head", split_axis=1, concat_axis=0, tiled=True),
    )
    blocks = part_keys.shape[0] // BLK
    query_blocks = part_queries.reshape(blocks, sub_rows, heads_dev, head_dim)
    key_blocks = part_keys.reshape(blocks, BLK, heads_dev, head_dim)
    value_blocks = part_values.reshape(blocks, BLK, heads_dev, head_dim)
    domains = lax.axis_size("dom")
    domain_here = lax.axis_index("dom")
    score_factor = head_dim ** (-0.5)
    own_rows = lax.dynamic_slice_in_dim(block_lists, domain_here * blocks, blocks, 0)
    near_ids = own_rows[:, :LC] - domain_here * blocks
    fold_width = min(8, domains - 1)
    capacity = (blocks * LE + fold_width - 1) // fold_width
    running = near_pass(query_blocks, key_blocks, value_blocks, near_ids, score_factor)

    def visit_turn(stride, loop_state):
        visitors, partial_value = loop_state
        visitors = from_behind(visitors, "dom", 1)
        partial_value = from_behind(
            (partial_value[0], partial_value[1], partial_value[2]), "dom", 1
        )
        source = (domain_here - stride) % domains
        far_rows = lax.dynamic_slice_in_dim(block_lists, source * blocks, blocks, 0)[:, LC:]
        partial_value = absorb(
            partial_value,
            visitors,
            far_rows,
            key_blocks,
            value_blocks,
            domain_here * blocks,
            capacity,
            score_factor,
        )
        return (visitors, partial_value)

    carried = lax.fori_loop(1, domains, visit_turn, (query_blocks, running))
    running = from_behind(carried[1], "dom", 1)
    summed, highest, totals = running
    attended = (
        (summed / totals[..., None]).astype(jnp.bfloat16).reshape(blocks * sub_rows, 1, head_cols)
    )
    regrouped = lax.all_to_all(attended, "head", split_axis=0, concat_axis=1, tiled=True)
    restored = (
        regrouped.reshape(local_blocks, sub_rows, groups, row_split, head_cols)
        .transpose(0, 3, 1, 2, 4)
        .reshape(node_rows, D)
    )
    return jnp.dot(restored, out_weight, preferred_element_type=jnp.float32).astype(jnp.bfloat16)


HALF = BLK // 2
PLANE = 4


def send_peer(me, step):
    z, rest = me // PLANE, me % PLANE
    i, j = step // PLANE, step % PLANE
    to_z = ((z // 2 + 1 - i // 2) % 2) * 2 + (z + i + i // 2) % 2
    return to_z * PLANE + (rest + 1 + j) % PLANE


def recv_peer(me, step):
    z, rest = me // PLANE, me % PLANE
    i, j = step // PLANE, step % PLANE
    from_z = ((z // 2 + 1 - i // 2) % 2) * 2 + (z + i + i // 2) % 2
    return from_z * PLANE + (rest + 3 - j) % PLANE


def swap_halves(x):
    return jnp.concatenate([x[:, HALF:], x[:, :HALF]], axis=1)


def low_lanes(shape):
    return lax.broadcasted_iota(jnp.int32, shape, 1) < HALF


def fused_kernel(
    lists, q_hbm, k_hbm, v_hbm, w_hbm, o_ref, q_ref, k_ref, v_ref,
    k_out, q_out, v_out, k_near, q_near, v_near, k_far, v_far, probs, att_out, att_in, w_ref,
    in_sem, k_send, k_recv, q_send, q_recv, v_send, v_recv, kf_send, kf_recv, vf_send, vf_recv, att_send, att_recv, w_sem,
):
    dom = lax.axis_index("dom")
    me = lax.axis_index("head")
    other = 1 - dom
    mesh_id = pl.DeviceIdType.MESH

    barrier = pltpu.get_barrier_semaphore()

    def greet(step, carry):
        pl.semaphore_signal(
            barrier, inc=1, device_id=(dom, send_peer(me, step)), device_id_type=mesh_id
        )
        return carry

    lax.fori_loop(0, HEADS - 1, greet, 0)
    pl.semaphore_signal(barrier, inc=1, device_id=(other, me), device_id_type=mesh_id)

    k_load = pltpu.make_async_copy(k_hbm, k_ref, in_sem.at[0])
    q_load = pltpu.make_async_copy(q_hbm, q_ref, in_sem.at[1])
    v_load = pltpu.make_async_copy(v_hbm, v_ref, in_sem.at[2])
    w_copy = pltpu.make_async_copy(w_hbm, w_ref, w_sem)
    k_load.start()
    q_load.start()
    v_load.start()
    w_copy.start()

    low = low_lanes((HALF, BLK))

    def pack(ref, pair):
        x = ref[:, pair * BLK : (pair + 1) * BLK]
        top, bottom = x[:HALF], x[HALF:]
        return (
            jnp.where(low, top, swap_halves(bottom)),
            jnp.where(low, swap_halves(top), bottom),
        )

    def pack_all(ref, out, factor):
        for pair in range(HEADS // 2):
            for odd, packed in enumerate(pack(ref, pair)):
                out[2 * pair + odd] = packed if factor is None else packed * jnp.bfloat16(factor)

    k_load.wait()
    pack_all(k_ref, k_out, None)
    pl.semaphore_wait(barrier, HEADS)

    def remote(src, dst, send, recv, device):
        return pltpu.make_async_remote_copy(
            src_ref=src, dst_ref=dst, send_sem=send, recv_sem=recv,
            device_id=device, device_id_type=mesh_id,
        )

    def k_copy(source, target):
        return remote(
            k_out.at[target], k_near.at[source], k_send.at[target], k_recv.at[source], (dom, target)
        )

    def q_copy(source, target):
        return remote(
            q_out.at[target], q_near.at[source], q_send.at[target], q_recv.at[source], (dom, target)
        )

    def v_copy(source, target):
        return remote(
            v_out.at[target], v_near.at[source], v_send.at[target], v_recv.at[source], (dom, target)
        )

    def kf_copy(block):
        return remote(
            k_near.at[block], k_far.at[block], kf_send.at[block], kf_recv.at[block], (other, me)
        )

    def vf_copy(block):
        return remote(
            v_near.at[block], v_far.at[block], vf_send.at[block], vf_recv.at[block], (other, me)
        )

    def att_copy(head, block):
        return remote(
            att_out.at[block], att_in.at[head], att_send.at[block], att_recv.at[head], (dom, block)
        )

    def send_k(step, carry):
        k_copy(me, send_peer(me, step)).start()
        return carry

    lax.fori_loop(0, HEADS - 1, send_k, 0)
    k_near[me] = k_out[me]
    kf_copy(me).start()

    q_load.wait()
    pack_all(q_ref, q_out, 0.125)

    def send_q(step, carry):
        q_copy(me, send_peer(me, step)).start()
        return carry

    lax.fori_loop(0, HEADS - 1, send_q, 0)
    q_near[me] = q_out[me]

    v_load.wait()
    pack_all(v_ref, v_out, None)
    v_near[me] = v_out[me]

    def pass_k(step, carry):
        source = recv_peer(me, step)
        k_copy(source, me).wait_recv()
        kf_copy(source).start()
        v_copy(me, send_peer(me, step)).start()
        return carry

    lax.fori_loop(0, HEADS - 1, pass_k, 0)
    vf_copy(me).start()

    def await_kf(block, carry):
        kf_copy(block).wait_recv()
        return carry

    lax.fori_loop(0, HEADS, await_kf, 0)

    def score_block(block):
        row = dom * HEADS + block
        keys = jnp.concatenate(
            [k_near[lax.rem(lists[c, row], HEADS)] for c in range(LC)]
            + [k_far[lax.rem(lists[c, row], HEADS)] for c in range(LC, LC + LE)],
            axis=0,
        )
        packed = q_near[block]
        swapped = swap_halves(packed)
        zero = jnp.zeros_like(packed)
        rows = jnp.concatenate(
            [
                jnp.where(low, packed, zero),
                jnp.where(low, swapped, zero),
                jnp.where(low, zero, swapped),
                jnp.where(low, zero, packed),
            ],
            axis=0,
        )
        scores = lax.dot_general(
            rows, keys, (((1,), (1,)), ((), ())), preferred_element_type=jnp.float32
        )
        folded = jnp.maximum(scores[:BLK], scores[BLK:])
        high = folded[:, :BLK]
        for at in range(BLK, (LC + LE) * HALF, BLK):
            high = jnp.maximum(high, folded[:, at : at + BLK])
        high = jnp.max(high, axis=1, keepdims=True)
        probs[block, :BLK, :] = jnp.exp(scores[:BLK] - high).astype(jnp.bfloat16)
        probs[block, BLK:, :] = jnp.exp(scores[BLK:] - high).astype(jnp.bfloat16)

    def score_and_pass(step, carry):
        source = recv_peer(me, step)
        q_copy(source, me).wait_recv()
        score_block(source)
        v_copy(source, me).wait_recv()
        vf_copy(source).start()
        return carry

    lax.fori_loop(0, HEADS - 1, score_and_pass, 0)
    score_block(me)

    def await_vf(block, carry):
        vf_copy(block).wait_recv()
        return carry

    lax.fori_loop(0, HEADS, await_vf, 0)

    def attend_block(block):
        row = dom * HEADS + block
        values = jnp.concatenate(
            [v_near[lax.rem(lists[c, row], HEADS)] for c in range(LC)]
            + [v_far[lax.rem(lists[c, row], HEADS)] for c in range(LC, LC + LE)],
            axis=0,
        )
        values = jnp.concatenate([values, jnp.ones_like(values)], axis=1)
        summed = jnp.dot(probs[block], values, preferred_element_type=jnp.float32)
        first, second = summed[:BLK, :BLK], summed[BLK:, :BLK]
        total = summed[:BLK, BLK:] + summed[BLK:, BLK:]
        total = jnp.where(low, total[:HALF], total[HALF:])
        packed = jnp.where(
            low,
            first[:HALF] + swap_halves(second[:HALF]),
            swap_halves(first[HALF:]) + second[HALF:],
        )
        return (packed / total).astype(jnp.bfloat16)

    def attend_and_send(step, carry):
        block = send_peer(me, step)
        att_out[block] = attend_block(block)
        att_copy(me, block).start()
        return carry

    lax.fori_loop(0, HEADS - 1, attend_and_send, 0)
    att_in[me] = attend_block(me)
    w_copy.wait()

    mixed = jnp.zeros((BLK, D), jnp.float32)
    for i in range(HEADS // PLANE):
        first_head = (recv_peer(me, i * PLANE) // PLANE) * PLANE
        for j in range(PLANE):
            head = first_head + j

            @pl.when(head != me)
            def _():
                att_copy(head, me).wait_recv()

        columns = []
        for j in range(0, PLANE, 2):
            even, odd = att_in[first_head + j], att_in[first_head + j + 1]
            columns.append(
                jnp.concatenate(
                    [
                        jnp.where(low, even, swap_halves(odd)),
                        jnp.where(low, swap_halves(even), odd),
                    ],
                    axis=0,
                )
            )
        attended = jnp.concatenate(columns, axis=1)
        rows_at = pl.multiple_of(first_head * HALF, PLANE * HALF)
        mixed = mixed + jnp.dot(
            attended, w_ref[pl.ds(rows_at, PLANE * HALF), :], preferred_element_type=jnp.float32
        )
    o_ref[...] = mixed.astype(o_ref.dtype)

    def settle(step, carry):
        target = send_peer(me, step)
        k_copy(me, target).wait_send()
        q_copy(me, target).wait_send()
        v_copy(me, target).wait_send()
        att_copy(me, target).wait_send()
        return carry

    lax.fori_loop(0, HEADS - 1, settle, 0)

    def settle_far(block, carry):
        kf_copy(block).wait_send()
        vf_copy(block).wait_send()
        return carry

    lax.fori_loop(0, HEADS, settle_far, 0)


def fused_shards(queries, key_vectors, value_vectors, block_lists, out_weight):
    vmem = pl.BlockSpec(memory_space=pltpu.VMEM)
    hbm = pl.BlockSpec(memory_space=pl.ANY)
    half_blocks = pltpu.VMEM((HEADS, HALF, BLK), jnp.bfloat16)
    pairs = HEADS * (LC + LE) * BLK * BLK
    return pl.pallas_call(
        fused_kernel,
        out_shape=jax.ShapeDtypeStruct(queries.shape, jnp.bfloat16),
        in_specs=[
            pl.BlockSpec(memory_space=pltpu.SMEM),
            hbm,
            hbm,
            hbm,
            hbm,
        ],
        out_specs=vmem,
        scratch_shapes=[pltpu.VMEM((BLK, D), jnp.bfloat16)] * 3
        + [half_blocks] * 8
        + [
            pltpu.VMEM((HEADS, 2 * BLK, (LC + LE) * HALF), jnp.bfloat16),
            half_blocks,
            half_blocks,
            pltpu.VMEM((D, D), jnp.bfloat16),
            pltpu.SemaphoreType.DMA((3,)),
        ]
        + [pltpu.SemaphoreType.DMA((HEADS,))] * 12
        + [pltpu.SemaphoreType.DMA],
        compiler_params=pltpu.CompilerParams(
            collective_id=0, has_side_effects=True, vmem_limit_bytes=60 * 1024 * 1024
        ),
        cost_estimate=pl.CostEstimate(
            flops=4 * pairs * (D // HEADS) + 2 * BLK * D * D,
            bytes_accessed=4 * BLK * D * 2 + D * D * 2,
            transcendentals=pairs,
        ),
    )(block_lists.T, queries, key_vectors, value_vectors, out_weight)


def solution(mesh):
    in_specs = (
        P(("dom", "head"), None),
        P(("dom", "head"), None),
        P(("dom", "head"), None),
        P(),
        P(),
    )
    out_specs = P(("dom", "head"), None)
    fused_fits = mesh.shape["dom"] == 2 and mesh.shape["head"] == HEADS
    body = fused_shards if fused_fits else shards
    return jax.shard_map(body, mesh=mesh, in_specs=in_specs, out_specs=out_specs, check_vma=False)
```

```python
import functools

import jax
import jax.numpy as jnp
from jax import lax
from jax.experimental import pallas as pl
from jax.experimental.pallas import tpu as pltpu
from jax.sharding import PartitionSpec as P

D = 1024
HEADS = 16
BLK = 128
LC = 4
LE = 8


lowest_value = -1e30


def from_behind(x, axis, by):
    devices = lax.axis_size(axis)
    return lax.ppermute(x, axis, [(i, (i + by) % devices) for i in range(devices)])


def attend(query_tiles, key_tiles, value_tiles, factor):
    tiles = key_tiles.shape[0]
    heads_dev = key_tiles.shape[2]
    head_dim = key_tiles.shape[3]
    listed_count = key_tiles.shape[1] // BLK
    key_parts = key_tiles.reshape(tiles, listed_count, BLK, heads_dev, head_dim)
    value_parts = value_tiles.reshape(tiles, listed_count, BLK, heads_dev, head_dim)
    scores = (
        jnp.einsum("tqhd,tlkhd->tqhlk", query_tiles, key_parts, preferred_element_type=jnp.float32)
        * factor
    )
    block_high = jnp.max(scores, axis=-1)
    highest = jnp.max(block_high, axis=-1)
    scale_back = jnp.exp(block_high - highest[..., None])
    weights = jnp.exp(scores - block_high[..., None])
    totals = jnp.sum(scale_back * jnp.sum(weights, axis=-1), axis=-1)
    per_block = jnp.einsum(
        "tqhlk,tlkhd->tqhld",
        weights.astype(jnp.bfloat16),
        value_parts,
        preferred_element_type=jnp.float32,
    )
    summed = jnp.sum(per_block * scale_back[..., None], axis=3)
    return (summed, highest, totals)


def near_pass(query_blocks, key_blocks, value_blocks, near_ids, factor):
    blocks, block_rows, heads_dev, head_dim = query_blocks.shape
    groups = blocks // 4

    def group_pass(operands):
        query_group, id_group = operands
        key_group = key_blocks[id_group].reshape(4, -1, heads_dev, head_dim)
        value_group = value_blocks[id_group].reshape(4, -1, heads_dev, head_dim)
        return attend(query_group, key_group, value_group, factor)

    summed, highest, totals = lax.map(
        group_pass,
        (
            query_blocks.reshape(groups, 4, block_rows, heads_dev, head_dim),
            near_ids.reshape(groups, 4, -1),
        ),
    )
    return (
        summed.reshape(blocks, block_rows, heads_dev, head_dim),
        highest.reshape(blocks, block_rows, heads_dev),
        totals.reshape(blocks, block_rows, heads_dev),
    )


def slot_table(listed, wanted, capacity):
    places = jnp.cumsum(wanted.astype(jnp.int32)) - 1
    tile_slots = jnp.arange(capacity, dtype=jnp.int32)
    taking = wanted[None, :] & (places[None, :] == tile_slots[:, None])
    filled = jnp.any(taking, axis=1)
    entries = jnp.arange(listed.shape[0], dtype=jnp.int32)
    chosen_entry = jnp.sum(jnp.where(taking, entries[None, :], 0), axis=1)
    chosen_block = jnp.sum(jnp.where(taking, listed[None, :], 0), axis=1)
    return (filled, chosen_entry, chosen_block)


def merge_tiles(running, tile_query, filled, tile_summed, tile_highest, tile_totals):
    summed, highest, totals = running
    blocks = summed.shape[0]
    member = (tile_query[None, :] == jnp.arange(blocks, dtype=jnp.int32)[:, None]) & filled[None, :]
    reached = jnp.max(jnp.where(member[:, :, None, None], tile_highest[None], lowest_value), axis=1)
    new_highest = jnp.maximum(highest, reached)
    rescale = jnp.where(filled[:, None, None], jnp.exp(tile_highest - new_highest[tile_query]), 0.0)
    retain = jnp.exp(highest - new_highest)
    member_float = member.astype(jnp.float32)
    totals = totals * retain + jnp.einsum(
        "qt,tbh->qbh", member_float, rescale * tile_totals, precision=lax.Precision.HIGHEST
    )
    summed = summed * retain[..., None] + jnp.einsum(
        "qt,tbhd->qbhd",
        member_float,
        rescale[..., None] * tile_summed,
        precision=lax.Precision.HIGHEST,
    )
    return (summed, new_highest, totals)


def absorb(running, query_blocks, far_ids, key_blocks, value_blocks, first_block, capacity, factor):
    reach_blocks = key_blocks.shape[0]
    listed = far_ids.reshape(-1)
    wanted = (listed >= first_block) & (listed < first_block + reach_blocks)
    filled, chosen_entry, chosen_block = slot_table(listed, wanted, capacity)
    tile_query = chosen_entry // far_ids.shape[1]
    tile_key = jnp.where(filled, chosen_block - first_block, 0)
    tile_summed, tile_highest, tile_totals = attend(
        query_blocks[tile_query], key_blocks[tile_key], value_blocks[tile_key], factor
    )
    return merge_tiles(running, tile_query, filled, tile_summed, tile_highest, tile_totals)


def shards(queries, key_vectors, value_vectors, block_lists, out_weight):
    node_rows = queries.shape[0]
    head_dim = D // HEADS
    head_devices = lax.axis_size("head")
    row_split = max(1, head_devices // HEADS)
    groups = head_devices // row_split
    heads_dev = HEADS // groups
    head_cols = heads_dev * head_dim
    local_blocks = node_rows // BLK
    sub_rows = BLK // row_split
    query_parts = (
        queries.reshape(local_blocks, row_split, sub_rows, groups, head_cols)
        .transpose(0, 2, 3, 1, 4)
        .reshape(local_blocks * sub_rows, groups * row_split, head_cols)
    )

    def spread(tensor):
        return jnp.broadcast_to(
            tensor.reshape(node_rows, groups, 1, head_cols),
            (node_rows, groups, row_split, head_cols),
        ).reshape(node_rows, groups * row_split, head_cols)

    part_queries, part_keys, part_values = (
        lax.all_to_all(query_parts, "head", split_axis=1, concat_axis=0, tiled=True),
        lax.all_to_all(spread(key_vectors), "head", split_axis=1, concat_axis=0, tiled=True),
        lax.all_to_all(spread(value_vectors), "head", split_axis=1, concat_axis=0, tiled=True),
    )
    blocks = part_keys.shape[0] // BLK
    query_blocks = part_queries.reshape(blocks, sub_rows, heads_dev, head_dim)
    key_blocks = part_keys.reshape(blocks, BLK, heads_dev, head_dim)
    value_blocks = part_values.reshape(blocks, BLK, heads_dev, head_dim)
    domains = lax.axis_size("dom")
    domain_here = lax.axis_index("dom")
    score_factor = head_dim ** (-0.5)
    own_rows = lax.dynamic_slice_in_dim(block_lists, domain_here * blocks, blocks, 0)
    near_ids = own_rows[:, :LC] - domain_here * blocks
    fold_width = min(8, domains - 1)
    capacity = (blocks * LE + fold_width - 1) // fold_width
    running = near_pass(query_blocks, key_blocks, value_blocks, near_ids, score_factor)

    def visit_turn(stride, loop_state):
        visitors, partial_value = loop_state
        visitors = from_behind(visitors, "dom", 1)
        partial_value = from_behind(
            (partial_value[0], partial_value[1], partial_value[2]), "dom", 1
        )
        source = (domain_here - stride) % domains
        far_rows = lax.dynamic_slice_in_dim(block_lists, source * blocks, blocks, 0)[:, LC:]
        partial_value = absorb(
            partial_value,
            visitors,
            far_rows,
            key_blocks,
            value_blocks,
            domain_here * blocks,
            capacity,
            score_factor,
        )
        return (visitors, partial_value)

    carried = lax.fori_loop(1, domains, visit_turn, (query_blocks, running))
    running = from_behind(carried[1], "dom", 1)
    summed, highest, totals = running
    attended = (
        (summed / totals[..., None]).astype(jnp.bfloat16).reshape(blocks * sub_rows, 1, head_cols)
    )
    regrouped = lax.all_to_all(attended, "head", split_axis=0, concat_axis=1, tiled=True)
    restored = (
        regrouped.reshape(local_blocks, sub_rows, groups, row_split, head_cols)
        .transpose(0, 3, 1, 2, 4)
        .reshape(node_rows, D)
    )
    return jnp.dot(restored, out_weight, preferred_element_type=jnp.float32).astype(jnp.bfloat16)


HALF = BLK // 2
PLANE = 4


def plane_at(me, turn):
    z = me // PLANE
    return ((z // 2 + 1 - turn // 2) % 2) * 2 + (z + turn + turn // 2) % 2


def send_peer(me, step):
    turn, place = step // PLANE, step % PLANE
    return plane_at(me, turn) * PLANE + (me % PLANE + 1 + place) % PLANE


def recv_peer(me, step):
    step = HEADS - 2 - step
    turn, place = step // PLANE, step % PLANE
    return plane_at(me, turn) * PLANE + (me % PLANE + 3 - place) % PLANE


def swap_halves(x):
    return jnp.concatenate([x[:, HALF:], x[:, :HALF]], axis=1)


def low_lanes(shape):
    return lax.broadcasted_iota(jnp.int32, shape, 1) < HALF


def fused_kernel(
    lists, q_hbm, k_hbm, v_hbm, w_hbm, o_ref, q_ref, k_ref, v_ref,
    k_out, q_out, v_out, k_near, q_near, v_near, k_far, v_far, probs, att_out, att_in, w_ref,
    in_sem, k_send, k_recv, q_send, q_recv, v_send, v_recv, kf_send, kf_recv, vf_send, vf_recv, att_send, att_recv, w_sem,
):
    dom = lax.axis_index("dom")
    me = lax.axis_index("head")
    other = 1 - dom
    mesh_id = pl.DeviceIdType.MESH

    barrier = pltpu.get_barrier_semaphore()

    def greet(step, carry):
        pl.semaphore_signal(
            barrier, inc=1, device_id=(dom, send_peer(me, step)), device_id_type=mesh_id
        )
        return carry

    for step in range(HEADS - 1):
        greet(step, 0)
    pl.semaphore_signal(barrier, inc=1, device_id=(other, me), device_id_type=mesh_id)

    k_load = pltpu.make_async_copy(k_hbm, k_ref, in_sem.at[0])
    q_load = pltpu.make_async_copy(q_hbm, q_ref, in_sem.at[1])
    v_load = pltpu.make_async_copy(v_hbm, v_ref, in_sem.at[2])
    w_copy = pltpu.make_async_copy(w_hbm, w_ref, w_sem)
    k_load.start()
    q_load.start()
    v_load.start()
    w_copy.start()

    low = low_lanes((HALF, BLK))

    def pack(ref, pair):
        x = ref[:, pair * BLK : (pair + 1) * BLK]
        top, bottom = x[:HALF], x[HALF:]
        return (
            jnp.where(low, top, swap_halves(bottom)),
            jnp.where(low, swap_halves(top), bottom),
        )

    def pack_all(ref, out, factor):
        for pair in range(HEADS // 2):
            for odd, packed in enumerate(pack(ref, pair)):
                out[2 * pair + odd] = packed if factor is None else packed * jnp.bfloat16(factor)

    k_load.wait()
    pack_all(k_ref, k_out, None)
    pl.semaphore_wait(barrier, HEADS)

    def remote(src, dst, send, recv, device):
        return pltpu.make_async_remote_copy(
            src_ref=src, dst_ref=dst, send_sem=send, recv_sem=recv,
            device_id=device, device_id_type=mesh_id,
        )

    def k_copy(source, target):
        return remote(
            k_out.at[target], k_near.at[source], k_send.at[target], k_recv.at[source], (dom, target)
        )

    def q_copy(source, target):
        return remote(
            q_out.at[target], q_near.at[source], q_send.at[target], q_recv.at[source], (dom, target)
        )

    def v_copy(source, target):
        return remote(
            v_out.at[target], v_near.at[source], v_send.at[target], v_recv.at[source], (dom, target)
        )

    def kf_copy(block):
        return remote(
            k_near.at[block], k_far.at[block], kf_send.at[block], kf_recv.at[block], (other, me)
        )

    def vf_copy(block):
        return remote(
            v_near.at[block], v_far.at[block], vf_send.at[block], vf_recv.at[block], (other, me)
        )

    def att_copy(head, block):
        return remote(
            att_out.at[block], att_in.at[head], att_send.at[block], att_recv.at[head], (dom, block)
        )

    def send_k(step, carry):
        k_copy(me, send_peer(me, step)).start()
        return carry

    lax.fori_loop(0, HEADS - 1, send_k, 0)
    k_near[me] = k_out[me]
    kf_copy(me).start()

    q_load.wait()
    pack_all(q_ref, q_out, 0.125)

    def send_q(step, carry):
        q_copy(me, send_peer(me, step)).start()
        return carry

    lax.fori_loop(0, HEADS - 1, send_q, 0)
    q_near[me] = q_out[me]

    v_load.wait()
    pack_all(v_ref, v_out, None)
    v_near[me] = v_out[me]

    def send_v(step, carry):
        v_copy(me, send_peer(me, step)).start()
        return carry

    lax.fori_loop(0, HEADS - 1, send_v, 0)

    def pass_k(step, carry):
        source = recv_peer(me, step)
        k_copy(source, me).wait_recv()
        kf_copy(source).start()
        return carry

    lax.fori_loop(0, HEADS - 1, pass_k, 0)
    vf_copy(me).start()

    def await_kf(block, carry):
        kf_copy(block).wait_recv()
        return carry

    lax.fori_loop(0, HEADS, await_kf, 0)

    def score_block(block):
        row = dom * HEADS + block
        keys = jnp.concatenate(
            [k_near[lax.rem(lists[c, row], HEADS)] for c in range(LC)]
            + [k_far[lax.rem(lists[c, row], HEADS)] for c in range(LC, LC + LE)],
            axis=0,
        )
        packed = q_near[block]
        swapped = swap_halves(packed)
        zero = jnp.zeros_like(packed)
        rows = jnp.concatenate(
            [
                jnp.where(low, packed, zero),
                jnp.where(low, swapped, zero),
                jnp.where(low, zero, swapped),
                jnp.where(low, zero, packed),
            ],
            axis=0,
        )
        scores = lax.dot_general(
            rows, keys, (((1,), (1,)), ((), ())), preferred_element_type=jnp.float32
        )
        folded = jnp.maximum(scores[:BLK], scores[BLK:])
        high = folded[:, :BLK]
        for at in range(BLK, (LC + LE) * HALF, BLK):
            high = jnp.maximum(high, folded[:, at : at + BLK])
        high = jnp.max(high, axis=1, keepdims=True)
        probs[block, :BLK, :] = jnp.exp(scores[:BLK] - high).astype(jnp.bfloat16)
        probs[block, BLK:, :] = jnp.exp(scores[BLK:] - high).astype(jnp.bfloat16)

    def score_and_pass(step, carry):
        source = recv_peer(me, step)
        q_copy(source, me).wait_recv()
        score_block(source)
        v_copy(source, me).wait_recv()
        vf_copy(source).start()
        return carry

    lax.fori_loop(0, HEADS - 1, score_and_pass, 0)
    score_block(me)

    def await_vf(block, carry):
        vf_copy(block).wait_recv()
        return carry

    lax.fori_loop(0, HEADS, await_vf, 0)

    def attend_block(block):
        row = dom * HEADS + block
        values = jnp.concatenate(
            [v_near[lax.rem(lists[c, row], HEADS)] for c in range(LC)]
            + [v_far[lax.rem(lists[c, row], HEADS)] for c in range(LC, LC + LE)],
            axis=0,
        )
        values = jnp.concatenate([values, jnp.ones_like(values)], axis=1)
        summed = jnp.dot(probs[block], values, preferred_element_type=jnp.float32)
        first, second = summed[:BLK, :BLK], summed[BLK:, :BLK]
        total = summed[:BLK, BLK:] + summed[BLK:, BLK:]
        total = jnp.where(low, total[:HALF], total[HALF:])
        packed = jnp.where(
            low,
            first[:HALF] + swap_halves(second[:HALF]),
            swap_halves(first[HALF:]) + second[HALF:],
        )
        return (packed / total).astype(jnp.bfloat16)

    def attend_and_send(step, carry):
        block = send_peer(me, step)
        att_out[block] = attend_block(block)
        att_copy(me, block).start()
        return carry

    lax.fori_loop(0, HEADS - 1, attend_and_send, 0)
    att_in[me] = attend_block(me)
    w_copy.wait()

    mixed = jnp.zeros((BLK, D), jnp.float32)
    for i in range(HEADS // PLANE):
        first_head = plane_at(me, i) * PLANE
        for j in range(PLANE):
            head = first_head + j

            @pl.when(head != me)
            def _():
                att_copy(head, me).wait_recv()

        columns = []
        for j in range(0, PLANE, 2):
            even, odd = att_in[first_head + j], att_in[first_head + j + 1]
            columns.append(
                jnp.concatenate(
                    [
                        jnp.where(low, even, swap_halves(odd)),
                        jnp.where(low, swap_halves(even), odd),
                    ],
                    axis=0,
                )
            )
        attended = jnp.concatenate(columns, axis=1)
        rows_at = pl.multiple_of(first_head * HALF, PLANE * HALF)
        mixed = mixed + jnp.dot(
            attended, w_ref[pl.ds(rows_at, PLANE * HALF), :], preferred_element_type=jnp.float32
        )
    o_ref[...] = mixed.astype(o_ref.dtype)

    def settle(step, carry):
        target = send_peer(me, step)
        k_copy(me, target).wait_send()
        q_copy(me, target).wait_send()
        v_copy(me, target).wait_send()
        att_copy(me, target).wait_send()
        return carry

    lax.fori_loop(0, HEADS - 1, settle, 0)

    def settle_far(block, carry):
        kf_copy(block).wait_send()
        vf_copy(block).wait_send()
        return carry

    lax.fori_loop(0, HEADS, settle_far, 0)


def fused_shards(queries, key_vectors, value_vectors, block_lists, out_weight):
    vmem = pl.BlockSpec(memory_space=pltpu.VMEM)
    hbm = pl.BlockSpec(memory_space=pl.ANY)
    half_blocks = pltpu.VMEM((HEADS, HALF, BLK), jnp.bfloat16)
    pairs = HEADS * (LC + LE) * BLK * BLK
    return pl.pallas_call(
        fused_kernel,
        out_shape=jax.ShapeDtypeStruct(queries.shape, jnp.bfloat16),
        in_specs=[
            pl.BlockSpec(memory_space=pltpu.SMEM),
            hbm,
            hbm,
            hbm,
            hbm,
        ],
        out_specs=vmem,
        scratch_shapes=[pltpu.VMEM((BLK, D), jnp.bfloat16)] * 3
        + [half_blocks] * 8
        + [
            pltpu.VMEM((HEADS, 2 * BLK, (LC + LE) * HALF), jnp.bfloat16),
            half_blocks,
            half_blocks,
            pltpu.VMEM((D, D), jnp.bfloat16),
            pltpu.SemaphoreType.DMA((3,)),
        ]
        + [pltpu.SemaphoreType.DMA((HEADS,))] * 12
        + [pltpu.SemaphoreType.DMA],
        compiler_params=pltpu.CompilerParams(
            collective_id=0, has_side_effects=True, vmem_limit_bytes=60 * 1024 * 1024
        ),
        cost_estimate=pl.CostEstimate(
            flops=4 * pairs * (D // HEADS) + 2 * BLK * D * D,
            bytes_accessed=4 * BLK * D * 2 + D * D * 2,
            transcendentals=pairs,
        ),
    )(block_lists.T, queries, key_vectors, value_vectors, out_weight)


def solution(mesh):
    in_specs = (
        P(("dom", "head"), None),
        P(("dom", "head"), None),
        P(("dom", "head"), None),
        P(),
        P(),
    )
    out_specs = P(("dom", "head"), None)
    fused_fits = mesh.shape["dom"] == 2 and mesh.shape["head"] == HEADS
    body = fused_shards if fused_fits else shards
    return jax.shard_map(body, mesh=mesh, in_specs=in_specs, out_specs=out_specs, check_vma=False)
```

```python
import functools

import jax
import jax.numpy as jnp
from jax import lax
from jax.experimental import pallas as pl
from jax.experimental.pallas import tpu as pltpu
from jax.sharding import PartitionSpec as P

D = 1024
HEADS = 16
BLK = 128
LC = 4
LE = 8


lowest_value = -1e30


def from_behind(x, axis, by):
    devices = lax.axis_size(axis)
    return lax.ppermute(x, axis, [(i, (i + by) % devices) for i in range(devices)])


def attend(query_tiles, key_tiles, value_tiles, factor):
    tiles = key_tiles.shape[0]
    heads_dev = key_tiles.shape[2]
    head_dim = key_tiles.shape[3]
    listed_count = key_tiles.shape[1] // BLK
    key_parts = key_tiles.reshape(tiles, listed_count, BLK, heads_dev, head_dim)
    value_parts = value_tiles.reshape(tiles, listed_count, BLK, heads_dev, head_dim)
    scores = (
        jnp.einsum("tqhd,tlkhd->tqhlk", query_tiles, key_parts, preferred_element_type=jnp.float32)
        * factor
    )
    block_high = jnp.max(scores, axis=-1)
    highest = jnp.max(block_high, axis=-1)
    scale_back = jnp.exp(block_high - highest[..., None])
    weights = jnp.exp(scores - block_high[..., None])
    totals = jnp.sum(scale_back * jnp.sum(weights, axis=-1), axis=-1)
    per_block = jnp.einsum(
        "tqhlk,tlkhd->tqhld",
        weights.astype(jnp.bfloat16),
        value_parts,
        preferred_element_type=jnp.float32,
    )
    summed = jnp.sum(per_block * scale_back[..., None], axis=3)
    return (summed, highest, totals)


def near_pass(query_blocks, key_blocks, value_blocks, near_ids, factor):
    blocks, block_rows, heads_dev, head_dim = query_blocks.shape
    groups = blocks // 4

    def group_pass(operands):
        query_group, id_group = operands
        key_group = key_blocks[id_group].reshape(4, -1, heads_dev, head_dim)
        value_group = value_blocks[id_group].reshape(4, -1, heads_dev, head_dim)
        return attend(query_group, key_group, value_group, factor)

    summed, highest, totals = lax.map(
        group_pass,
        (
            query_blocks.reshape(groups, 4, block_rows, heads_dev, head_dim),
            near_ids.reshape(groups, 4, -1),
        ),
    )
    return (
        summed.reshape(blocks, block_rows, heads_dev, head_dim),
        highest.reshape(blocks, block_rows, heads_dev),
        totals.reshape(blocks, block_rows, heads_dev),
    )


def slot_table(listed, wanted, capacity):
    places = jnp.cumsum(wanted.astype(jnp.int32)) - 1
    tile_slots = jnp.arange(capacity, dtype=jnp.int32)
    taking = wanted[None, :] & (places[None, :] == tile_slots[:, None])
    filled = jnp.any(taking, axis=1)
    entries = jnp.arange(listed.shape[0], dtype=jnp.int32)
    chosen_entry = jnp.sum(jnp.where(taking, entries[None, :], 0), axis=1)
    chosen_block = jnp.sum(jnp.where(taking, listed[None, :], 0), axis=1)
    return (filled, chosen_entry, chosen_block)


def merge_tiles(running, tile_query, filled, tile_summed, tile_highest, tile_totals):
    summed, highest, totals = running
    blocks = summed.shape[0]
    member = (tile_query[None, :] == jnp.arange(blocks, dtype=jnp.int32)[:, None]) & filled[None, :]
    reached = jnp.max(jnp.where(member[:, :, None, None], tile_highest[None], lowest_value), axis=1)
    new_highest = jnp.maximum(highest, reached)
    rescale = jnp.where(filled[:, None, None], jnp.exp(tile_highest - new_highest[tile_query]), 0.0)
    retain = jnp.exp(highest - new_highest)
    member_float = member.astype(jnp.float32)
    totals = totals * retain + jnp.einsum(
        "qt,tbh->qbh", member_float, rescale * tile_totals, precision=lax.Precision.HIGHEST
    )
    summed = summed * retain[..., None] + jnp.einsum(
        "qt,tbhd->qbhd",
        member_float,
        rescale[..., None] * tile_summed,
        precision=lax.Precision.HIGHEST,
    )
    return (summed, new_highest, totals)


def absorb(running, query_blocks, far_ids, key_blocks, value_blocks, first_block, capacity, factor):
    reach_blocks = key_blocks.shape[0]
    listed = far_ids.reshape(-1)
    wanted = (listed >= first_block) & (listed < first_block + reach_blocks)
    filled, chosen_entry, chosen_block = slot_table(listed, wanted, capacity)
    tile_query = chosen_entry // far_ids.shape[1]
    tile_key = jnp.where(filled, chosen_block - first_block, 0)
    tile_summed, tile_highest, tile_totals = attend(
        query_blocks[tile_query], key_blocks[tile_key], value_blocks[tile_key], factor
    )
    return merge_tiles(running, tile_query, filled, tile_summed, tile_highest, tile_totals)


def shards(queries, key_vectors, value_vectors, block_lists, out_weight):
    node_rows = queries.shape[0]
    head_dim = D // HEADS
    head_devices = lax.axis_size("head")
    row_split = max(1, head_devices // HEADS)
    groups = head_devices // row_split
    heads_dev = HEADS // groups
    head_cols = heads_dev * head_dim
    local_blocks = node_rows // BLK
    sub_rows = BLK // row_split
    query_parts = (
        queries.reshape(local_blocks, row_split, sub_rows, groups, head_cols)
        .transpose(0, 2, 3, 1, 4)
        .reshape(local_blocks * sub_rows, groups * row_split, head_cols)
    )

    def spread(tensor):
        return jnp.broadcast_to(
            tensor.reshape(node_rows, groups, 1, head_cols),
            (node_rows, groups, row_split, head_cols),
        ).reshape(node_rows, groups * row_split, head_cols)

    part_queries, part_keys, part_values = (
        lax.all_to_all(query_parts, "head", split_axis=1, concat_axis=0, tiled=True),
        lax.all_to_all(spread(key_vectors), "head", split_axis=1, concat_axis=0, tiled=True),
        lax.all_to_all(spread(value_vectors), "head", split_axis=1, concat_axis=0, tiled=True),
    )
    blocks = part_keys.shape[0] // BLK
    query_blocks = part_queries.reshape(blocks, sub_rows, heads_dev, head_dim)
    key_blocks = part_keys.reshape(blocks, BLK, heads_dev, head_dim)
    value_blocks = part_values.reshape(blocks, BLK, heads_dev, head_dim)
    domains = lax.axis_size("dom")
    domain_here = lax.axis_index("dom")
    score_factor = head_dim ** (-0.5)
    own_rows = lax.dynamic_slice_in_dim(block_lists, domain_here * blocks, blocks, 0)
    near_ids = own_rows[:, :LC] - domain_here * blocks
    fold_width = min(8, domains - 1)
    capacity = (blocks * LE + fold_width - 1) // fold_width
    running = near_pass(query_blocks, key_blocks, value_blocks, near_ids, score_factor)

    def visit_turn(stride, loop_state):
        visitors, partial_value = loop_state
        visitors = from_behind(visitors, "dom", 1)
        partial_value = from_behind(
            (partial_value[0], partial_value[1], partial_value[2]), "dom", 1
        )
        source = (domain_here - stride) % domains
        far_rows = lax.dynamic_slice_in_dim(block_lists, source * blocks, blocks, 0)[:, LC:]
        partial_value = absorb(
            partial_value,
            visitors,
            far_rows,
            key_blocks,
            value_blocks,
            domain_here * blocks,
            capacity,
            score_factor,
        )
        return (visitors, partial_value)

    carried = lax.fori_loop(1, domains, visit_turn, (query_blocks, running))
    running = from_behind(carried[1], "dom", 1)
    summed, highest, totals = running
    attended = (
        (summed / totals[..., None]).astype(jnp.bfloat16).reshape(blocks * sub_rows, 1, head_cols)
    )
    regrouped = lax.all_to_all(attended, "head", split_axis=0, concat_axis=1, tiled=True)
    restored = (
        regrouped.reshape(local_blocks, sub_rows, groups, row_split, head_cols)
        .transpose(0, 3, 1, 2, 4)
        .reshape(node_rows, D)
    )
    return jnp.dot(restored, out_weight, preferred_element_type=jnp.float32).astype(jnp.bfloat16)


HALF = BLK // 2
PLANE = 4


def chip_at(me, turn, place):
    x, z, y = me // 8, (me // 2) % 4, me % 2
    to_z = ((z // 2 + 1 - turn // 2) % 2) * 2 + (z + turn + turn // 2) % 2
    spot = (x * 2 + y + place) % PLANE
    return (spot // 2) * 8 + to_z * 2 + spot % 2


def send_peer(me, step):
    return chip_at(me, step // PLANE, 1 + step % PLANE)


def recv_peer(me, step):
    step = HEADS - 2 - step
    return chip_at(me, step // PLANE, 3 - step % PLANE)


def swap_halves(x):
    return jnp.concatenate([x[:, HALF:], x[:, :HALF]], axis=1)


def low_lanes(shape):
    return lax.broadcasted_iota(jnp.int32, shape, 1) < HALF


def fused_kernel(
    lists, q_hbm, k_hbm, v_hbm, w_hbm, o_ref, q_ref, k_ref, v_ref,
    k_out, q_out, v_out, q_near, k_all, v_all, probs, att_out, att_in, w_ref,
    in_sem, k_send, k_recv, q_send, q_recv, v_send, v_recv, kf_send, kf_recv, vf_send, vf_recv, att_send, att_recv, w_sem,
):
    core = lax.axis_index("head") % 2
    me = lax.axis_index("dom") * 8 + lax.axis_index("head") // 2

    def device(chip, on_core):
        return (chip // 8, (chip % 8) * 2 + on_core)

    def mine(chip):
        return chip * 2 + core

    sibling = device(me, 1 - core)
    mesh_id = pl.DeviceIdType.MESH

    barrier = pltpu.get_barrier_semaphore()

    def greet(step, carry):
        pl.semaphore_signal(
            barrier, inc=1, device_id=device(send_peer(me, step), core), device_id_type=mesh_id
        )
        return carry

    for step in range(HEADS - 1):
        greet(step, 0)
    pl.semaphore_signal(barrier, inc=1, device_id=sibling, device_id_type=mesh_id)

    k_load = pltpu.make_async_copy(k_hbm, k_ref, in_sem.at[0])
    q_load = pltpu.make_async_copy(q_hbm, q_ref, in_sem.at[1])
    v_load = pltpu.make_async_copy(v_hbm, v_ref, in_sem.at[2])
    w_copy = pltpu.make_async_copy(w_hbm, w_ref, w_sem)
    k_load.start()
    q_load.start()
    v_load.start()
    w_copy.start()

    low = low_lanes((HALF, BLK))

    def pack(ref, pair):
        x = ref[:, pair * BLK : (pair + 1) * BLK]
        top, bottom = x[:HALF], x[HALF:]
        return (
            jnp.where(low, top, swap_halves(bottom)),
            jnp.where(low, swap_halves(top), bottom),
        )

    def pack_all(ref, out, factor):
        for pair in range(HEADS // 2):
            for odd, packed in enumerate(pack(ref, pair)):
                out[2 * pair + odd] = packed if factor is None else packed * jnp.bfloat16(factor)

    k_load.wait()
    pack_all(k_ref, k_out, None)
    pl.semaphore_wait(barrier, HEADS)

    def remote(src, dst, send, recv, target):
        return pltpu.make_async_remote_copy(
            src_ref=src, dst_ref=dst, send_sem=send, recv_sem=recv,
            device_id=target, device_id_type=mesh_id,
        )

    def k_copy(source, target):
        return remote(
            k_out.at[target], k_all.at[mine(source)], k_send.at[target], k_recv.at[source],
            device(target, core),
        )

    def q_copy(source, target):
        return remote(
            q_out.at[target], q_near.at[source], q_send.at[target], q_recv.at[source],
            device(target, core),
        )

    def v_copy(source, target):
        return remote(
            v_out.at[target], v_all.at[mine(source)], v_send.at[target], v_recv.at[source],
            device(target, core),
        )

    def kf_copy(chip, on_core):
        block = chip * 2 + on_core
        return remote(
            k_all.at[block], k_all.at[block], kf_send.at[chip], kf_recv.at[chip], sibling
        )

    def vf_copy(chip, on_core):
        block = chip * 2 + on_core
        return remote(
            v_all.at[block], v_all.at[block], vf_send.at[chip], vf_recv.at[chip], sibling
        )

    def att_copy(head, target):
        return remote(
            att_out.at[target], att_in.at[head], att_send.at[target], att_recv.at[head],
            device(target, core),
        )

    def send_k(step, carry):
        k_copy(me, send_peer(me, step)).start()
        return carry

    lax.fori_loop(0, HEADS - 1, send_k, 0)
    k_all[mine(me)] = k_out[me]
    kf_copy(me, core).start()

    q_load.wait()
    pack_all(q_ref, q_out, 0.125)

    def send_q(step, carry):
        q_copy(me, send_peer(me, step)).start()
        return carry

    lax.fori_loop(0, HEADS - 1, send_q, 0)
    q_near[me] = q_out[me]

    v_load.wait()
    pack_all(v_ref, v_out, None)
    v_all[mine(me)] = v_out[me]

    def send_v(step, carry):
        v_copy(me, send_peer(me, step)).start()
        return carry

    lax.fori_loop(0, HEADS - 1, send_v, 0)

    def pass_k(step, carry):
        source = recv_peer(me, step)
        k_copy(source, me).wait_recv()
        kf_copy(source, core).start()
        return carry

    lax.fori_loop(0, HEADS - 1, pass_k, 0)
    vf_copy(me, core).start()

    def await_kf(block, carry):
        kf_copy(block, 1 - core).wait_recv()
        return carry

    lax.fori_loop(0, HEADS, await_kf, 0)

    def score_block(block):
        row = mine(block)
        keys = jnp.concatenate(
            [k_all[lists[c, row]] for c in range(LC + LE)], axis=0
        )
        packed = q_near[block]
        swapped = swap_halves(packed)
        zero = jnp.zeros_like(packed)
        rows = jnp.concatenate(
            [
                jnp.where(low, packed, zero),
                jnp.where(low, swapped, zero),
                jnp.where(low, zero, swapped),
                jnp.where(low, zero, packed),
            ],
            axis=0,
        )
        scores = lax.dot_general(
            rows, keys, (((1,), (1,)), ((), ())), preferred_element_type=jnp.float32
        )
        folded = jnp.maximum(scores[:BLK], scores[BLK:])
        high = folded[:, :BLK]
        for at in range(BLK, (LC + LE) * HALF, BLK):
            high = jnp.maximum(high, folded[:, at : at + BLK])
        high = jnp.max(high, axis=1, keepdims=True)
        probs[block, :BLK, :] = jnp.exp(scores[:BLK] - high).astype(jnp.bfloat16)
        probs[block, BLK:, :] = jnp.exp(scores[BLK:] - high).astype(jnp.bfloat16)

    def score_and_pass(step, carry):
        source = recv_peer(me, step)
        q_copy(source, me).wait_recv()
        score_block(source)
        v_copy(source, me).wait_recv()
        vf_copy(source, core).start()
        return carry

    lax.fori_loop(0, HEADS - 1, score_and_pass, 0)
    score_block(me)

    def await_vf(block, carry):
        vf_copy(block, 1 - core).wait_recv()
        return carry

    lax.fori_loop(0, HEADS, await_vf, 0)

    def attend_block(block):
        row = mine(block)
        values = jnp.concatenate(
            [v_all[lists[c, row]] for c in range(LC + LE)], axis=0
        )
        values = jnp.concatenate([values, jnp.ones_like(values)], axis=1)
        summed = jnp.dot(probs[block], values, preferred_element_type=jnp.float32)
        first, second = summed[:BLK, :BLK], summed[BLK:, :BLK]
        total = summed[:BLK, BLK:] + summed[BLK:, BLK:]
        total = jnp.where(low, total[:HALF], total[HALF:])
        packed = jnp.where(
            low,
            first[:HALF] + swap_halves(second[:HALF]),
            swap_halves(first[HALF:]) + second[HALF:],
        )
        return (packed / total).astype(jnp.bfloat16)

    def attend_and_send(step, carry):
        block = send_peer(me, step)
        att_out[block] = attend_block(block)
        att_copy(me, block).start()
        return carry

    lax.fori_loop(0, HEADS - 1, attend_and_send, 0)
    att_in[me] = attend_block(me)
    w_copy.wait()

    mixed = jnp.zeros((BLK, D), jnp.float32)
    for turn in range(HEADS // PLANE):
        columns, weight_rows = [], []
        for x in range(2):
            first = (chip_at(me, turn, 0) // 2 % 4) * 2 + x * 8
            for head in (first, first + 1):

                @pl.when(head != me)
                def _():
                    att_copy(head, me).wait_recv()

            even, odd = att_in[first], att_in[first + 1]
            columns.append(
                jnp.concatenate(
                    [
                        jnp.where(low, even, swap_halves(odd)),
                        jnp.where(low, swap_halves(even), odd),
                    ],
                    axis=0,
                )
            )
            rows_at = pl.multiple_of(first * HALF, BLK)
            weight_rows.append(w_ref[pl.ds(rows_at, BLK), :])
        mixed = mixed + jnp.dot(
            jnp.concatenate(columns, axis=1),
            jnp.concatenate(weight_rows, axis=0),
            preferred_element_type=jnp.float32,
        )
    o_ref[...] = mixed.astype(o_ref.dtype)

    def settle(step, carry):
        target = send_peer(me, step)
        k_copy(me, target).wait_send()
        q_copy(me, target).wait_send()
        v_copy(me, target).wait_send()
        att_copy(me, target).wait_send()
        return carry

    lax.fori_loop(0, HEADS - 1, settle, 0)

    def settle_far(block, carry):
        kf_copy(block, core).wait_send()
        vf_copy(block, core).wait_send()
        return carry

    lax.fori_loop(0, HEADS, settle_far, 0)


def fused_shards(queries, key_vectors, value_vectors, block_lists, out_weight):
    vmem = pl.BlockSpec(memory_space=pltpu.VMEM)
    hbm = pl.BlockSpec(memory_space=pl.ANY)
    half_blocks = pltpu.VMEM((HEADS, HALF, BLK), jnp.bfloat16)
    pairs = HEADS * (LC + LE) * BLK * BLK
    return pl.pallas_call(
        fused_kernel,
        out_shape=jax.ShapeDtypeStruct(queries.shape, jnp.bfloat16),
        in_specs=[
            pl.BlockSpec(memory_space=pltpu.SMEM),
            hbm,
            hbm,
            hbm,
            hbm,
        ],
        out_specs=vmem,
        scratch_shapes=[pltpu.VMEM((BLK, D), jnp.bfloat16)] * 3
        + [half_blocks] * 4
        + [pltpu.VMEM((2 * HEADS, HALF, BLK), jnp.bfloat16)] * 2
        + [
            pltpu.VMEM((HEADS, 2 * BLK, (LC + LE) * HALF), jnp.bfloat16),
            half_blocks,
            half_blocks,
            pltpu.VMEM((D, D), jnp.bfloat16),
            pltpu.SemaphoreType.DMA((3,)),
        ]
        + [pltpu.SemaphoreType.DMA((HEADS,))] * 12
        + [pltpu.SemaphoreType.DMA],
        compiler_params=pltpu.CompilerParams(
            collective_id=0, has_side_effects=True, vmem_limit_bytes=60 * 1024 * 1024
        ),
        cost_estimate=pl.CostEstimate(
            flops=4 * pairs * (D // HEADS) + 2 * BLK * D * D,
            bytes_accessed=4 * BLK * D * 2 + D * D * 2,
            transcendentals=pairs,
        ),
    )(block_lists.T, queries, key_vectors, value_vectors, out_weight)


def solution(mesh):
    in_specs = (
        P(("dom", "head"), None),
        P(("dom", "head"), None),
        P(("dom", "head"), None),
        P(),
        P(),
    )
    out_specs = P(("dom", "head"), None)
    fused_fits = mesh.shape["dom"] == 2 and mesh.shape["head"] == HEADS
    body = fused_shards if fused_fits else shards
    return jax.shard_map(body, mesh=mesh, in_specs=in_specs, out_specs=out_specs, check_vma=False)
```

```python
import functools

import jax
import jax.numpy as jnp
from jax import lax
from jax.experimental import pallas as pl
from jax.experimental.pallas import tpu as pltpu
from jax.sharding import PartitionSpec as P

D = 1024
HEADS = 16
BLK = 128
LC = 4
LE = 8


lowest_value = -1e30


def from_behind(x, axis, by):
    devices = lax.axis_size(axis)
    return lax.ppermute(x, axis, [(i, (i + by) % devices) for i in range(devices)])


def attend(query_tiles, key_tiles, value_tiles, factor):
    tiles = key_tiles.shape[0]
    heads_dev = key_tiles.shape[2]
    head_dim = key_tiles.shape[3]
    listed_count = key_tiles.shape[1] // BLK
    key_parts = key_tiles.reshape(tiles, listed_count, BLK, heads_dev, head_dim)
    value_parts = value_tiles.reshape(tiles, listed_count, BLK, heads_dev, head_dim)
    scores = (
        jnp.einsum("tqhd,tlkhd->tqhlk", query_tiles, key_parts, preferred_element_type=jnp.float32)
        * factor
    )
    block_high = jnp.max(scores, axis=-1)
    highest = jnp.max(block_high, axis=-1)
    scale_back = jnp.exp(block_high - highest[..., None])
    weights = jnp.exp(scores - block_high[..., None])
    totals = jnp.sum(scale_back * jnp.sum(weights, axis=-1), axis=-1)
    per_block = jnp.einsum(
        "tqhlk,tlkhd->tqhld",
        weights.astype(jnp.bfloat16),
        value_parts,
        preferred_element_type=jnp.float32,
    )
    summed = jnp.sum(per_block * scale_back[..., None], axis=3)
    return (summed, highest, totals)


def near_pass(query_blocks, key_blocks, value_blocks, near_ids, factor):
    blocks, block_rows, heads_dev, head_dim = query_blocks.shape
    groups = blocks // 4

    def group_pass(operands):
        query_group, id_group = operands
        key_group = key_blocks[id_group].reshape(4, -1, heads_dev, head_dim)
        value_group = value_blocks[id_group].reshape(4, -1, heads_dev, head_dim)
        return attend(query_group, key_group, value_group, factor)

    summed, highest, totals = lax.map(
        group_pass,
        (
            query_blocks.reshape(groups, 4, block_rows, heads_dev, head_dim),
            near_ids.reshape(groups, 4, -1),
        ),
    )
    return (
        summed.reshape(blocks, block_rows, heads_dev, head_dim),
        highest.reshape(blocks, block_rows, heads_dev),
        totals.reshape(blocks, block_rows, heads_dev),
    )


def slot_table(listed, wanted, capacity):
    places = jnp.cumsum(wanted.astype(jnp.int32)) - 1
    tile_slots = jnp.arange(capacity, dtype=jnp.int32)
    taking = wanted[None, :] & (places[None, :] == tile_slots[:, None])
    filled = jnp.any(taking, axis=1)
    entries = jnp.arange(listed.shape[0], dtype=jnp.int32)
    chosen_entry = jnp.sum(jnp.where(taking, entries[None, :], 0), axis=1)
    chosen_block = jnp.sum(jnp.where(taking, listed[None, :], 0), axis=1)
    return (filled, chosen_entry, chosen_block)


def merge_tiles(running, tile_query, filled, tile_summed, tile_highest, tile_totals):
    summed, highest, totals = running
    blocks = summed.shape[0]
    member = (tile_query[None, :] == jnp.arange(blocks, dtype=jnp.int32)[:, None]) & filled[None, :]
    reached = jnp.max(jnp.where(member[:, :, None, None], tile_highest[None], lowest_value), axis=1)
    new_highest = jnp.maximum(highest, reached)
    rescale = jnp.where(filled[:, None, None], jnp.exp(tile_highest - new_highest[tile_query]), 0.0)
    retain = jnp.exp(highest - new_highest)
    member_float = member.astype(jnp.float32)
    totals = totals * retain + jnp.einsum(
        "qt,tbh->qbh", member_float, rescale * tile_totals, precision=lax.Precision.HIGHEST
    )
    summed = summed * retain[..., None] + jnp.einsum(
        "qt,tbhd->qbhd",
        member_float,
        rescale[..., None] * tile_summed,
        precision=lax.Precision.HIGHEST,
    )
    return (summed, new_highest, totals)


def absorb(running, query_blocks, far_ids, key_blocks, value_blocks, first_block, capacity, factor):
    reach_blocks = key_blocks.shape[0]
    listed = far_ids.reshape(-1)
    wanted = (listed >= first_block) & (listed < first_block + reach_blocks)
    filled, chosen_entry, chosen_block = slot_table(listed, wanted, capacity)
    tile_query = chosen_entry // far_ids.shape[1]
    tile_key = jnp.where(filled, chosen_block - first_block, 0)
    tile_summed, tile_highest, tile_totals = attend(
        query_blocks[tile_query], key_blocks[tile_key], value_blocks[tile_key], factor
    )
    return merge_tiles(running, tile_query, filled, tile_summed, tile_highest, tile_totals)


def shards(queries, key_vectors, value_vectors, block_lists, out_weight):
    node_rows = queries.shape[0]
    head_dim = D // HEADS
    head_devices = lax.axis_size("head")
    row_split = max(1, head_devices // HEADS)
    groups = head_devices // row_split
    heads_dev = HEADS // groups
    head_cols = heads_dev * head_dim
    local_blocks = node_rows // BLK
    sub_rows = BLK // row_split
    query_parts = (
        queries.reshape(local_blocks, row_split, sub_rows, groups, head_cols)
        .transpose(0, 2, 3, 1, 4)
        .reshape(local_blocks * sub_rows, groups * row_split, head_cols)
    )

    def spread(tensor):
        return jnp.broadcast_to(
            tensor.reshape(node_rows, groups, 1, head_cols),
            (node_rows, groups, row_split, head_cols),
        ).reshape(node_rows, groups * row_split, head_cols)

    part_queries, part_keys, part_values = (
        lax.all_to_all(query_parts, "head", split_axis=1, concat_axis=0, tiled=True),
        lax.all_to_all(spread(key_vectors), "head", split_axis=1, concat_axis=0, tiled=True),
        lax.all_to_all(spread(value_vectors), "head", split_axis=1, concat_axis=0, tiled=True),
    )
    blocks = part_keys.shape[0] // BLK
    query_blocks = part_queries.reshape(blocks, sub_rows, heads_dev, head_dim)
    key_blocks = part_keys.reshape(blocks, BLK, heads_dev, head_dim)
    value_blocks = part_values.reshape(blocks, BLK, heads_dev, head_dim)
    domains = lax.axis_size("dom")
    domain_here = lax.axis_index("dom")
    score_factor = head_dim ** (-0.5)
    own_rows = lax.dynamic_slice_in_dim(block_lists, domain_here * blocks, blocks, 0)
    near_ids = own_rows[:, :LC] - domain_here * blocks
    fold_width = min(8, domains - 1)
    capacity = (blocks * LE + fold_width - 1) // fold_width
    running = near_pass(query_blocks, key_blocks, value_blocks, near_ids, score_factor)

    def visit_turn(stride, loop_state):
        visitors, partial_value = loop_state
        visitors = from_behind(visitors, "dom", 1)
        partial_value = from_behind(
            (partial_value[0], partial_value[1], partial_value[2]), "dom", 1
        )
        source = (domain_here - stride) % domains
        far_rows = lax.dynamic_slice_in_dim(block_lists, source * blocks, blocks, 0)[:, LC:]
        partial_value = absorb(
            partial_value,
            visitors,
            far_rows,
            key_blocks,
            value_blocks,
            domain_here * blocks,
            capacity,
            score_factor,
        )
        return (visitors, partial_value)

    carried = lax.fori_loop(1, domains, visit_turn, (query_blocks, running))
    running = from_behind(carried[1], "dom", 1)
    summed, highest, totals = running
    attended = (
        (summed / totals[..., None]).astype(jnp.bfloat16).reshape(blocks * sub_rows, 1, head_cols)
    )
    regrouped = lax.all_to_all(attended, "head", split_axis=0, concat_axis=1, tiled=True)
    restored = (
        regrouped.reshape(local_blocks, sub_rows, groups, row_split, head_cols)
        .transpose(0, 3, 1, 2, 4)
        .reshape(node_rows, D)
    )
    return jnp.dot(restored, out_weight, preferred_element_type=jnp.float32).astype(jnp.bfloat16)


HALF = BLK // 2
PLANE = 4


def chip_at(me, turn, place):
    x, z, y = me // 8, (me // 2) % 4, me % 2
    to_z = ((z // 2 + 1 - turn // 2) % 2) * 2 + (z + turn + turn // 2) % 2
    spot = (x * 2 + y + place) % PLANE
    return (spot // 2) * 8 + to_z * 2 + spot % 2


def send_peer(me, step):
    return chip_at(me, step // PLANE, 1 + step % PLANE)


def recv_peer(me, step):
    step = HEADS - 2 - step
    return chip_at(me, step // PLANE, 3 - step % PLANE)


def swap_halves(x):
    return jnp.concatenate([x[:, HALF:], x[:, :HALF]], axis=1)


def low_lanes(shape):
    return lax.broadcasted_iota(jnp.int32, shape, 1) < HALF


def fused_kernel(
    lists, q_hbm, k_hbm, v_hbm, w_hbm, o_ref, q_ref, k_ref, v_ref,
    k_out, q_out, v_out, q_near, k_all, v_all, probs, att_out, att_in, w_ref,
    in_sem, k_send, k_recv, q_send, q_recv, v_send, v_recv, kf_send, kf_recv, vf_send, vf_recv, att_send, att_recv, w_sem,
):
    core = lax.axis_index("head") % 2
    me = lax.axis_index("dom") * 8 + lax.axis_index("head") // 2

    def device(chip, on_core):
        return (chip // 8, (chip % 8) * 2 + on_core)

    def mine(chip):
        return chip * 2 + core

    sibling = device(me, 1 - core)
    mesh_id = pl.DeviceIdType.MESH

    barrier = pltpu.get_barrier_semaphore()

    def greet(step, carry):
        pl.semaphore_signal(
            barrier, inc=1, device_id=device(send_peer(me, step), core), device_id_type=mesh_id
        )
        return carry

    for step in range(HEADS - 1):
        greet(step, 0)
    pl.semaphore_signal(barrier, inc=1, device_id=sibling, device_id_type=mesh_id)

    k_load = pltpu.make_async_copy(k_hbm, k_ref, in_sem.at[0])
    q_load = pltpu.make_async_copy(q_hbm, q_ref, in_sem.at[1])
    v_load = pltpu.make_async_copy(v_hbm, v_ref, in_sem.at[2])
    w_copy = pltpu.make_async_copy(w_hbm, w_ref, w_sem)
    k_load.start()
    q_load.start()
    v_load.start()
    w_copy.start()

    low = low_lanes((HALF, BLK))

    def pack(ref, pair):
        x = ref[:, pair * BLK : (pair + 1) * BLK]
        top, bottom = x[:HALF], x[HALF:]
        return (
            jnp.where(low, top, swap_halves(bottom)),
            jnp.where(low, swap_halves(top), bottom),
        )

    def pack_all(ref, out, factor):
        for pair in range(HEADS // 2):
            for odd, packed in enumerate(pack(ref, pair)):
                out[2 * pair + odd] = packed if factor is None else packed * jnp.bfloat16(factor)

    k_load.wait()
    pack_all(k_ref, k_out, None)
    pl.semaphore_wait(barrier, HEADS)

    def remote(src, dst, send, recv, target):
        return pltpu.make_async_remote_copy(
            src_ref=src, dst_ref=dst, send_sem=send, recv_sem=recv,
            device_id=target, device_id_type=mesh_id,
        )

    def k_copy(source, target):
        return remote(
            k_out.at[target], k_all.at[mine(source)], k_send.at[target], k_recv.at[source],
            device(target, core),
        )

    def q_copy(source, target):
        return remote(
            q_out.at[target], q_near.at[source], q_send.at[target], q_recv.at[source],
            device(target, core),
        )

    def v_copy(source, target):
        return remote(
            v_out.at[target], v_all.at[mine(source)], v_send.at[target], v_recv.at[source],
            device(target, core),
        )

    def kf_copy(chip, on_core):
        block = chip * 2 + on_core
        return remote(
            k_all.at[block], k_all.at[block], kf_send.at[chip], kf_recv.at[chip], sibling
        )

    def vf_copy(chip, on_core):
        block = chip * 2 + on_core
        return remote(
            v_all.at[block], v_all.at[block], vf_send.at[chip], vf_recv.at[chip], sibling
        )

    def att_copy(head, target):
        return remote(
            att_out.at[target], att_in.at[head], att_send.at[target], att_recv.at[head],
            device(target, core),
        )

    def send_k(step, carry):
        k_copy(me, send_peer(me, step)).start()
        return carry

    for step in range(HEADS - 1):
        send_k(step, 0)
    k_all[mine(me)] = k_out[me]
    kf_copy(me, core).start()

    q_load.wait()
    pack_all(q_ref, q_out, 0.125)

    def send_q(step, carry):
        q_copy(me, send_peer(me, step)).start()
        return carry

    for step in range(HEADS - 1):
        send_q(step, 0)
    q_near[me] = q_out[me]

    v_load.wait()
    pack_all(v_ref, v_out, None)
    v_all[mine(me)] = v_out[me]

    def send_v(step, carry):
        v_copy(me, send_peer(me, step)).start()
        return carry

    for step in range(HEADS - 1):
        send_v(step, 0)

    def pass_k(step, carry):
        source = recv_peer(me, step)
        k_copy(source, me).wait_recv()
        kf_copy(source, core).start()
        return carry

    lax.fori_loop(0, HEADS - 1, pass_k, 0)
    vf_copy(me, core).start()

    def await_kf(block, carry):
        kf_copy(block, 1 - core).wait_recv()
        return carry

    lax.fori_loop(0, HEADS, await_kf, 0)

    def score_block(block):
        row = mine(block)
        keys = jnp.concatenate(
            [k_all[lists[c, row]] for c in range(LC + LE)], axis=0
        )
        packed = q_near[block]
        swapped = swap_halves(packed)
        zero = jnp.zeros_like(packed)
        rows = jnp.concatenate(
            [
                jnp.where(low, packed, zero),
                jnp.where(low, swapped, zero),
                jnp.where(low, zero, swapped),
                jnp.where(low, zero, packed),
            ],
            axis=0,
        )
        scores = lax.dot_general(
            rows, keys, (((1,), (1,)), ((), ())), preferred_element_type=jnp.float32
        )
        folded = jnp.maximum(scores[:BLK], scores[BLK:])
        high = folded[:, :BLK]
        for at in range(BLK, (LC + LE) * HALF, BLK):
            high = jnp.maximum(high, folded[:, at : at + BLK])
        high = jnp.max(high, axis=1, keepdims=True)
        probs[block, :BLK, :] = jnp.exp(scores[:BLK] - high).astype(jnp.bfloat16)
        probs[block, BLK:, :] = jnp.exp(scores[BLK:] - high).astype(jnp.bfloat16)

    def score_and_pass(step, carry):
        source = recv_peer(me, step)
        q_copy(source, me).wait_recv()
        score_block(source)
        v_copy(source, me).wait_recv()
        vf_copy(source, core).start()
        return carry

    lax.fori_loop(0, HEADS - 1, score_and_pass, 0)
    score_block(me)

    def await_vf(block, carry):
        vf_copy(block, 1 - core).wait_recv()
        return carry

    lax.fori_loop(0, HEADS, await_vf, 0)

    def attend_block(block):
        row = mine(block)
        values = jnp.concatenate(
            [v_all[lists[c, row]] for c in range(LC + LE)], axis=0
        )
        values = jnp.concatenate([values, jnp.ones_like(values)], axis=1)
        summed = jnp.dot(probs[block], values, preferred_element_type=jnp.float32)
        first, second = summed[:BLK, :BLK], summed[BLK:, :BLK]
        total = summed[:BLK, BLK:] + summed[BLK:, BLK:]
        total = jnp.where(low, total[:HALF], total[HALF:])
        packed = jnp.where(
            low,
            first[:HALF] + swap_halves(second[:HALF]),
            swap_halves(first[HALF:]) + second[HALF:],
        )
        return (packed / total).astype(jnp.bfloat16)

    def attend_and_send(step, carry):
        block = send_peer(me, step)
        att_out[block] = attend_block(block)
        att_copy(me, block).start()
        return carry

    lax.fori_loop(0, HEADS - 1, attend_and_send, 0)
    att_in[me] = attend_block(me)
    w_copy.wait()

    def settle(step, carry):
        target = send_peer(me, step)
        k_copy(me, target).wait_send()
        q_copy(me, target).wait_send()
        v_copy(me, target).wait_send()
        return carry

    lax.fori_loop(0, HEADS - 1, settle, 0)

    def settle_far(block, carry):
        kf_copy(block, core).wait_send()
        vf_copy(block, core).wait_send()
        return carry

    lax.fori_loop(0, HEADS, settle_far, 0)

    mixed = jnp.zeros((BLK, D), jnp.float32)
    for turn in range(HEADS // PLANE):
        columns, weight_rows = [], []
        for x in range(2):
            first = (chip_at(me, turn, 0) // 2 % 4) * 2 + x * 8
            for head in (first, first + 1):

                @pl.when(head != me)
                def _():
                    att_copy(head, me).wait_recv()

            even, odd = att_in[first], att_in[first + 1]
            columns.append(
                jnp.concatenate(
                    [
                        jnp.where(low, even, swap_halves(odd)),
                        jnp.where(low, swap_halves(even), odd),
                    ],
                    axis=0,
                )
            )
            rows_at = pl.multiple_of(first * HALF, BLK)
            weight_rows.append(w_ref[pl.ds(rows_at, BLK), :])
        mixed = mixed + jnp.dot(
            jnp.concatenate(columns, axis=1),
            jnp.concatenate(weight_rows, axis=0),
            preferred_element_type=jnp.float32,
        )
    q_ref[...] = mixed.astype(q_ref.dtype)
    o_copy = pltpu.make_async_copy(q_ref, o_ref, in_sem.at[0])
    o_copy.start()

    def settle_att(step, carry):
        att_copy(me, send_peer(me, step)).wait_send()
        return carry

    lax.fori_loop(0, HEADS - 1, settle_att, 0)
    o_copy.wait()


def fused_shards(queries, key_vectors, value_vectors, block_lists, out_weight):
    vmem = pl.BlockSpec(memory_space=pltpu.VMEM)
    hbm = pl.BlockSpec(memory_space=pl.ANY)
    half_blocks = pltpu.VMEM((HEADS, HALF, BLK), jnp.bfloat16)
    pairs = HEADS * (LC + LE) * BLK * BLK
    return pl.pallas_call(
        fused_kernel,
        out_shape=jax.ShapeDtypeStruct(queries.shape, jnp.bfloat16),
        in_specs=[
            pl.BlockSpec(memory_space=pltpu.SMEM),
            hbm,
            hbm,
            hbm,
            hbm,
        ],
        out_specs=hbm,
        scratch_shapes=[pltpu.VMEM((BLK, D), jnp.bfloat16)] * 3
        + [half_blocks] * 4
        + [pltpu.VMEM((2 * HEADS, HALF, BLK), jnp.bfloat16)] * 2
        + [
            pltpu.VMEM((HEADS, 2 * BLK, (LC + LE) * HALF), jnp.bfloat16),
            half_blocks,
            half_blocks,
            pltpu.VMEM((D, D), jnp.bfloat16),
            pltpu.SemaphoreType.DMA((3,)),
        ]
        + [pltpu.SemaphoreType.DMA((HEADS,))] * 12
        + [pltpu.SemaphoreType.DMA],
        compiler_params=pltpu.CompilerParams(
            collective_id=0, has_side_effects=True, vmem_limit_bytes=60 * 1024 * 1024
        ),
        cost_estimate=pl.CostEstimate(
            flops=4 * pairs * (D // HEADS) + 2 * BLK * D * D,
            bytes_accessed=4 * BLK * D * 2 + D * D * 2,
            transcendentals=pairs,
        ),
    )(block_lists.T, queries, key_vectors, value_vectors, out_weight)


def solution(mesh):
    in_specs = (
        P(("dom", "head"), None),
        P(("dom", "head"), None),
        P(("dom", "head"), None),
        P(),
        P(),
    )
    out_specs = P(("dom", "head"), None)
    fused_fits = mesh.shape["dom"] == 2 and mesh.shape["head"] == HEADS
    body = fused_shards if fused_fits else shards
    return jax.shard_map(body, mesh=mesh, in_specs=in_specs, out_specs=out_specs, check_vma=False)
```
